128 devices in a mesh: row: 8 (over z, core), col: 16 (over y, x).
Axes of the slice: x: 4, y: 4, z: 4, core: 2. Of those that a mesh axis runs over, the one named last changes fastest.
Arguments:
- object_field: float32 [2, 4096, 8192], P(None, 'row', 'col'), may hold values from -5 to 5
- illumination: float32 [2, 256, 256], replicated, may hold values from -5 to 5
- positions: int32 [4096, 2], P(('row', 'col')), may hold values from 0 to 511
- owners: int32 [4096], P(('row', 'col')), may hold values from 0 to 15, as said below
- intensities: float32 [4096, 256, 256], P(('row', 'col')), may hold values from 0.2 to 5
Outputs:
- object_grad: float32 [2, 4096, 8192], P(None, 'row', 'col')
- probe_grad: float32 [2, 256, 256], replicated
The draws below stay inside these ranges and needn't reach their ends.
Inputs may be any that keep to these rules, and one draw needn't show every extreme that they name: `owners`: position p belongs to the device block p // 32. In each block no owner column is named more than 3 times, and in every tile row one owner column is named exactly 3 times by every block of that row.
All inputs are finite; a program needn't handle non-finite values.
Results may differ from the reference program's by a relative error of at most 0.004.
The reference program's roundings to bfloat16 on the way count: a program that leaves them out, or rounds other values in their place, can miss the bound.
Values sent between devices are 32-bit elements; how exact they have to be, the bound alone decides.
A program may use at most 256 MiB of HBM per device.

```python
import math
import jax
import jax.numpy as jnp
from jax import lax

PATCH = 256
TILE = 512
POS_DEV = 32
ROW_TILES = 8
COL_TILES = 16
OBJ_R = 4096
OBJ_C = 8192
POSITIONS = 4096
CAP = 3


def draw_owners(key, part):
    key = jax.random.fold_in(key, 7)
    hot_key, block_key = jax.random.split(key)
    hot_cols = jax.random.randint(hot_key, (ROW_TILES,), 0, COL_TILES)
    block_total = ROW_TILES * COL_TILES
    block_keys = jax.random.split(block_key, block_total)
    band_of = jnp.arange(block_total, dtype=jnp.int32) // COL_TILES

    def one_block(block_rng, hot_col):
        first_key, second_key = jax.random.split(block_rng)
        others = jnp.arange((COL_TILES - 1) * CAP, dtype=jnp.int32) // CAP
        others = jax.random.permutation(first_key, others)[:POS_DEV - CAP]
        others = others + (others >= hot_col).astype(jnp.int32)
        listed = jnp.concatenate([jnp.full((CAP,), hot_col, jnp.int32), others])
        return jax.random.permutation(second_key, listed)
    return jax.vmap(one_block)(block_keys, hot_cols[band_of]).reshape(-1)


def touch_ends(array, own_key, least, high):
    longest = array.shape.index(max(array.shape))
    spots = []
    for shift in (0, 1):
        where = [jax.random.randint(jax.random.fold_in(own_key, axis), (), 0, length) for axis, length in enumerate(array.shape)]
        where[longest] = (where[longest] + shift) % array.shape[longest]
        spots.append(tuple(where))
    return array.at[spots[0]].set(least).at[spots[1]].set(high)


def level_of(rng, dims, pieces, least, top_value):
    gain, own = 1.0, jax.random.fold_in(rng, 6)
    for axis_at, shards_of in pieces:
        steps = jnp.exp(jax.random.uniform(jax.random.fold_in(own, axis_at), (shards_of,), jnp.float32, least / len(pieces), top_value / len(pieces)))
        gain = gain * jnp.repeat(steps, dims[axis_at] // shards_of).reshape([-1 if axis == axis_at else 1 for axis in range(len(dims))])
    return gain


def gaussian(own_key, extent, width, reach, pieces=(), kind=jnp.bfloat16):
    values = jax.random.normal(own_key, extent, jnp.float32) * width
    if len(pieces) > 0:
        values = level_of(own_key, extent, pieces, -0.22, 0.18) * values
    return jnp.clip(values, min=-reach, max=reach).astype(kind)


def setup_inputs(seed: int = 0) -> dict:
    arg_keys = jax.random.split(jax.random.key(seed), 6)
    object_field = gaussian(arg_keys[0], (2, OBJ_R, OBJ_C), 0.7, 5.0, ((1, 8), (2, 16)), jnp.float32)
    illumination = gaussian(arg_keys[1], (2, PATCH, PATCH), 0.7, 5.0, (), jnp.float32)
    positions = touch_ends(jax.random.randint(arg_keys[2], (POSITIONS, 2), 0, TILE), jax.random.fold_in(arg_keys[2], 1), 0, TILE - 1).astype(jnp.int32)
    owners = draw_owners(jax.random.fold_in(arg_keys[5], 71), 0)
    intensities = jnp.clip(jnp.exp(math.log(5.0) - 3.218876 * jax.random.uniform(arg_keys[4], (POSITIONS, PATCH, PATCH), jnp.float32) ** level_of(arg_keys[4], (POSITIONS, PATCH, PATCH), ((0, 128),), -0.2, 0.2)), 0.2, 5.0)
    return dict(object_field=object_field, illumination=illumination, positions=positions, owners=owners, intensities=intensities)


def dft_tables(length):
    grid_ids = jnp.arange(length, dtype=jnp.int32)
    phase_ids = grid_ids[:, None] * grid_ids[None, :] % length
    angles = phase_ids.astype(jnp.float32) * (2.0 * math.pi / length)
    scale_factor = 1.0 / math.sqrt(length)
    return ((jnp.cos(angles) * scale_factor).astype(jnp.bfloat16), (-jnp.sin(angles) * scale_factor).astype(jnp.bfloat16))

def product(first, second):
    return jnp.dot(first, second, preferred_element_type=jnp.float32)

def transform(real_part, imag_part, table_re, table_im):
    mid_re = (product(table_re, real_part) - product(table_im, imag_part)).astype(jnp.bfloat16)
    mid_im = (product(table_re, imag_part) + product(table_im, real_part)).astype(jnp.bfloat16)
    out_re = product(mid_re, table_re) - product(mid_im, table_im)
    out_im = product(mid_re, table_im) + product(mid_im, table_re)
    return (out_re, out_im)

def residual_wave(patch_now, illumination, measured, table_re, table_im):
    exit_re = (illumination[0] * patch_now[0] - illumination[1] * patch_now[1]).astype(jnp.bfloat16)
    exit_im = (illumination[0] * patch_now[1] + illumination[1] * patch_now[0]).astype(jnp.bfloat16)
    wave_re, wave_im = transform(exit_re, exit_im, table_re, table_im)
    amplitude = jnp.sqrt(wave_re * wave_re + wave_im * wave_im)
    factor = 1.0 - jnp.sqrt(measured) / jnp.maximum(amplitude, 0.5)
    diff_re = (wave_re * factor).astype(jnp.bfloat16)
    diff_im = (wave_im * factor).astype(jnp.bfloat16)
    return transform(diff_re, diff_im, table_re, -table_im)

def reference(object_field, illumination, positions, owners, intensities):
    position_ids = jnp.arange(POSITIONS, dtype=jnp.int32)
    band_rows = position_ids // (POS_DEV * COL_TILES)
    top_rows = jnp.minimum(band_rows * TILE + positions[:, 0], OBJ_R - PATCH).astype(jnp.int32)
    left_cols = jnp.minimum(owners * TILE + positions[:, 1], OBJ_C - PATCH).astype(jnp.int32)
    table_re, table_im = dft_tables(PATCH)
    anchor = jnp.zeros((), jnp.int32)

    def accumulate(totals, record):
        object_total, probe_total = totals
        row_at, col_at, measured = record
        patch_now = lax.dynamic_slice(object_field, (anchor, row_at, col_at), (2, PATCH, PATCH))
        back_re, back_im = residual_wave(patch_now, illumination, measured, table_re, table_im)
        object_term = jnp.stack([illumination[0] * back_re + illumination[1] * back_im, illumination[0] * back_im - illumination[1] * back_re])
        window = lax.dynamic_slice(object_total, (anchor, row_at, col_at), (2, PATCH, PATCH)) + object_term
        object_total = lax.dynamic_update_slice(object_total, window, (anchor, row_at, col_at))
        probe_total = probe_total + jnp.stack([patch_now[0] * back_re + patch_now[1] * back_im, patch_now[0] * back_im - patch_now[1] * back_re])
        return ((object_total, probe_total), None)
    initial = (jnp.zeros(object_field.shape, jnp.float32), jnp.zeros(illumination.shape, jnp.float32))
    (object_grad, probe_grad), _ = lax.scan(accumulate, initial, (top_rows, left_cols, intensities))
    return (object_grad, probe_grad / math.sqrt(POSITIONS))
```

```python
import functools
import math

import jax
import jax.numpy as jnp
from jax import lax
from jax.experimental import pallas as pl
from jax.experimental.pallas import tpu as pltpu
from jax.sharding import PartitionSpec as P

CAP = 3
LANES = 128


def passed_along(value, axis, steps):
    count = lax.axis_size(axis)
    leading, last = (max(0, -steps), min(count, count - steps))
    return lax.ppermute(value, axis, [(source, source + steps) for source in range(leading, last)])


def dft_tables(length):
    grid_ids = jnp.arange(length, dtype=jnp.int32)
    phase_ids = grid_ids[:, None] * grid_ids[None, :] % length
    angles = phase_ids.astype(jnp.float32) * (2.0 * math.pi / length)
    scale_factor = 1.0 / math.sqrt(length)
    return (
        (jnp.cos(angles) * scale_factor).astype(jnp.bfloat16),
        (-jnp.sin(angles) * scale_factor).astype(jnp.bfloat16),
    )


def pack_kernel(cap, slot_ref, src_ref, *refs):
    outs, sem = refs[:cap], refs[cap]
    count = src_ref.shape[0]

    def copy(p, layer, dest):
        return pltpu.make_async_copy(src_ref.at[p], outs[layer].at[dest], sem.at[p])

    def start(p, carry):
        slot = slot_ref[p]
        dest = slot // cap
        layer = slot - dest * cap
        for k in range(cap):

            @pl.when(layer == k)
            def _():
                copy(p, k, dest).start()

        return carry

    lax.fori_loop(0, count, start, 0)

    def finish(p, carry):
        copy(p, 0, 0).wait()
        return carry

    lax.fori_loop(0, count, finish, 0)


def pack(slot_of, intensities, cap, cols):
    plane = intensities.shape[1:]
    return pl.pallas_call(
        functools.partial(pack_kernel, cap),
        out_shape=[jax.ShapeDtypeStruct((cols,) + plane, jnp.float32)] * cap,
        in_specs=[
            pl.BlockSpec(memory_space=pltpu.SMEM),
            pl.BlockSpec(memory_space=pl.ANY),
        ],
        out_specs=[pl.BlockSpec(memory_space=pl.ANY)] * cap,
        scratch_shapes=[pltpu.SemaphoreType.DMA((slot_of.shape[0],))],
    )(slot_of, intensities)


def mm(first, second):
    return jnp.dot(first, second, preferred_element_type=jnp.float32)


def grad_kernel(
    first_call,
    meta_ref,
    main_ref,
    below_ref,
    beside_ref,
    illum_ref,
    left_ref,
    right_ref,
    meas_ref,
    grad_in,
    probe_in,
    grad_out,
    probe_out,
    ext,
    grad,
    probe,
    meas,
    patch_buf,
    live_list,
    load_sem,
    meas_sem,
    grad_sem,
):
    tile = main_ref.shape[1]
    side = illum_ref.shape[1]
    strips = ext.shape[1]
    main_strips = tile // LANES
    slots = meta_ref.shape[1]
    loads = []

    def load(src, dst):
        copy = pltpu.make_async_copy(src, dst, load_sem.at[len(loads)])
        copy.start()
        loads.append(copy)

    for c in range(2):
        for j in range(main_strips):
            lanes = pl.ds(j * LANES, LANES)
            load(main_ref.at[c, :, lanes], ext.at[c, j, pl.ds(0, tile)])
            load(below_ref.at[c, :, lanes], ext.at[c, j, pl.ds(tile, side)])
        for j in range(strips - main_strips):
            load(beside_ref.at[c, :, pl.ds(j * LANES, LANES)], ext.at[c, main_strips + j])
    if first_call:
        grad[...] = jnp.zeros(grad.shape, grad.dtype)
        probe[...] = jnp.zeros(probe.shape, probe.dtype)
    else:
        pre = pltpu.make_async_copy(grad_in, grad, grad_sem)
        pre.start()
        probe[...] = probe_in[...]

    def gather_live(s, n):
        alive = meta_ref[2, s] > 0

        @pl.when(alive)
        def _():
            live_list[n] = s

        return n + alive.astype(jnp.int32)

    total = lax.fori_loop(0, slots, gather_live, jnp.int32(0))

    def fetch(n):
        return pltpu.make_async_copy(meas_ref.at[live_list[n]], meas.at[n % 2], meas_sem.at[n % 2])

    @pl.when(total > 0)
    def _():
        fetch(0).start()

    for copy in loads:
        copy.wait()
    if not first_call:
        pre.wait()

    lane = lax.broadcasted_iota(jnp.int32, (side, LANES), 1)

    def step(n, carry):
        @pl.when(n + 1 < total)
        def _():
            fetch(n + 1).start()

        s = live_list[n]
        row = meta_ref[0, s]
        col = meta_ref[1, s]
        strip = col // LANES
        shift = col - strip * LANES
        back_shift = (LANES - shift) % LANES
        rows = pl.ds(row, side)
        keep = lane < LANES - shift
        for c in range(2):
            rolled = [pltpu.roll(ext[c, strip + t, rows, :], back_shift, 1) for t in range(3)]
            for t in range(2):
                patch_buf[c, :, pl.ds(t * LANES, LANES)] = jnp.where(keep, rolled[t], rolled[t + 1])
        il_re, il_im = illum_ref[0], illum_ref[1]
        pa_re, pa_im = patch_buf[0], patch_buf[1]
        exit_wave = jnp.concatenate(
            [
                (il_re * pa_re - il_im * pa_im).astype(jnp.bfloat16),
                (il_re * pa_im + il_im * pa_re).astype(jnp.bfloat16),
            ],
            axis=0,
        )
        forward, backward = left_ref[...], right_ref[...]
        mid = mm(forward, exit_wave).astype(jnp.bfloat16)
        wave = mm(jnp.concatenate([mid[:side], mid[side:]], axis=1), backward)
        w_re, w_im = wave[:, :side], wave[:, side:]
        fetch(n).wait()
        measured = meas[n % 2]
        power = jnp.maximum(w_re * w_re + w_im * w_im, 0.25)
        factor = 1.0 - measured * lax.rsqrt(measured * power)
        diff = jnp.concatenate(
            [(w_re * factor).astype(jnp.bfloat16), (w_im * factor).astype(jnp.bfloat16)], axis=0
        )
        mid = mm(backward, diff).astype(jnp.bfloat16)
        back = mm(jnp.concatenate([mid[:side], mid[side:]], axis=1), forward)
        b_re, b_im = back[:, :side], back[:, side:]
        pa_re, pa_im = patch_buf[0], patch_buf[1]
        probe[0] += pa_re * b_re + pa_im * b_im
        probe[1] += pa_re * b_im - pa_im * b_re
        terms = (il_re * b_re + il_im * b_im, il_re * b_im - il_im * b_re)
        early = lane < shift
        for c in range(2):
            first = pltpu.roll(terms[c][:, :LANES], shift, 1)
            second = pltpu.roll(terms[c][:, LANES:], shift, 1)
            grad[c, strip, rows, :] += jnp.where(early, 0.0, first)
            grad[c, strip + 1, rows, :] += jnp.where(early, first, second)
            grad[c, strip + 2, rows, :] += jnp.where(early, second, 0.0)
        return carry

    lax.fori_loop(0, total, step, 0)
    post = pltpu.make_async_copy(grad, grad_out, grad_sem)
    post.start()
    probe_out[...] = probe[...]
    post.wait()


def add_chunk(meta, pieces, illumination, tables, measured, grad, probe, first_call):
    main, below, beside = pieces
    tile, side = main.shape[1], illumination.shape[1]
    strips = (tile + side) // LANES
    grad_shape = (2, strips, tile + side, LANES)
    count = measured.shape[0]
    vmem = pl.BlockSpec(memory_space=pltpu.VMEM)
    smem = pl.BlockSpec(memory_space=pltpu.SMEM)
    hbm = pl.BlockSpec(memory_space=pl.ANY)
    return pl.pallas_call(
        functools.partial(grad_kernel, first_call),
        out_shape=[
            jax.ShapeDtypeStruct(grad_shape, jnp.float32),
            jax.ShapeDtypeStruct((2, side, side), jnp.float32),
        ],
        in_specs=[smem, hbm, hbm, hbm, vmem, vmem, vmem, hbm, hbm, vmem],
        out_specs=[hbm, vmem],
        scratch_shapes=[
            pltpu.VMEM(grad_shape, jnp.float32),
            pltpu.VMEM(grad_shape, jnp.float32),
            pltpu.VMEM((2, side, side), jnp.float32),
            pltpu.VMEM((2, side, side), jnp.float32),
            pltpu.VMEM((2, side, side), jnp.float32),
            pltpu.SMEM((count,), jnp.int32),
            pltpu.SemaphoreType.DMA((4 * strips,)),
            pltpu.SemaphoreType.DMA((2,)),
            pltpu.SemaphoreType.DMA,
        ],
        compiler_params=pltpu.CompilerParams(vmem_limit_bytes=40 * 2**20),
        cost_estimate=pl.CostEstimate(
            flops=count * 16 * 2 * side**3,
            bytes_accessed=count * 4 * side * side + 3 * 8 * (tile + side) ** 2,
            transcendentals=count * side * side,
        ),
    )(meta, main, below, beside, illumination, *tables, measured, grad, probe)


def on_device(object_field, illumination, positions, owners, intensities):
    tile = object_field.shape[1]
    side = illumination.shape[1]
    cols = lax.axis_size("col")
    row_count = lax.axis_size("row")
    pos_dev = positions.shape[0]
    band = lax.axis_index("row")
    column = lax.axis_index("col")
    limit_rows = row_count * tile - side
    limit_cols = cols * tile - side

    hits = (owners[:, None] == jnp.arange(cols, dtype=jnp.int32)[None, :]).astype(jnp.int32)
    earlier = jnp.sum((jnp.cumsum(hits, axis=0) - hits) * hits, axis=1)
    slot_of = owners * CAP + earlier
    layers = list(pack(slot_of, intensities, CAP, cols))
    request = jnp.stack([positions[:, 0], positions[:, 1], jnp.ones((pos_dev,), jnp.int32)], axis=1)
    chosen = (slot_of[:, None] == jnp.arange(cols * CAP, dtype=jnp.int32)[None, :]).astype(jnp.int32)
    request_buf = jnp.sum(chosen[:, :, None] * request[:, None, :], axis=0)
    got = lax.all_to_all(request_buf, "col", split_axis=0, concat_axis=0, tiled=True)
    row_at = jnp.minimum(band * tile + got[:, 0], limit_rows) - band * tile
    col_at = jnp.minimum(column * tile + got[:, 1], limit_cols) - column * tile
    meta = jnp.stack([row_at, col_at, got[:, 2]]).reshape(3, cols, CAP)

    below = passed_along(object_field[:, :side, :], "row", -1)
    taller = jnp.concatenate([object_field[:, :, :side], below[:, :, :side]], axis=1)
    beside = passed_along(taller, "col", -1)
    pieces = (object_field, below, beside)

    t_re, t_im = dft_tables(side)
    forward = jnp.block([[t_re, -t_im], [t_im, t_re]])
    backward = jnp.block([[t_re, t_im], [-t_im, t_re]])

    grad = jnp.zeros((2, (tile + side) // LANES, tile + side, LANES), jnp.float32)
    probe = jnp.zeros((2, side, side), jnp.float32)
    for k in range(CAP):
        arrived = lax.all_to_all(layers[k], "col", split_axis=0, concat_axis=0, tiled=True)
        if k + 1 < CAP:
            layers[k + 1], arrived = lax.optimization_barrier((layers[k + 1], arrived))
        grad, probe = add_chunk(
            meta[:, :, k], pieces, illumination, (forward, backward), arrived, grad, probe, k == 0
        )

    probe_total = lax.psum(probe, ("row", "col"))
    probe_grad = probe_total / math.sqrt(pos_dev * row_count * cols)

    plane = jnp.swapaxes(grad, 1, 2).reshape(2, tile + side, tile + side)
    from_left = passed_along(plane[:, :, tile:], "col", 1)
    merged = plane[:, :, :tile].at[:, :, :side].add(from_left)
    from_above = passed_along(merged[:, tile:, :], "row", 1)
    object_grad = merged[:, :tile, :].at[:, :side, :].add(from_above)
    return (object_grad, probe_grad)


def solution(mesh):
    return jax.shard_map(
        on_device,
        mesh=mesh,
        in_specs=(
            P(None, "row", "col"),
            P(),
            P(("row", "col"), None),
            P(("row", "col")),
            P(("row", "col"), None, None),
        ),
        out_specs=(P(None, "row", "col"), P()),
        check_vma=False,
    )
```

```python
import functools
import math

import jax
import jax.numpy as jnp
from jax import lax
from jax.experimental import pallas as pl
from jax.experimental.pallas import tpu as pltpu
from jax.sharding import PartitionSpec as P

CAP = 3
LANES = 128


def passed_along(value, axis, steps):
    count = lax.axis_size(axis)
    leading, last = (max(0, -steps), min(count, count - steps))
    return lax.ppermute(value, axis, [(source, source + steps) for source in range(leading, last)])


def dft_tables(length):
    grid_ids = jnp.arange(length, dtype=jnp.int32)
    phase_ids = grid_ids[:, None] * grid_ids[None, :] % length
    angles = phase_ids.astype(jnp.float32) * (2.0 * math.pi / length)
    scale_factor = 1.0 / math.sqrt(length)
    return (
        (jnp.cos(angles) * scale_factor).astype(jnp.bfloat16),
        (-jnp.sin(angles) * scale_factor).astype(jnp.bfloat16),
    )


def pack_kernel(layer_ref, dest_ref, src_ref, pair_out, last_out, held, in_sem, out_sem):
    count = src_ref.shape[0]

    def copy_in(p):
        return pltpu.make_async_copy(src_ref.at[p], held.at[p], in_sem.at[p])

    def copy_out(p, out):
        return pltpu.make_async_copy(held.at[p], out.at[dest_ref[p]], out_sem.at[p])

    for p in range(count):
        copy_in(p).start()
    for p in range(count):
        copy_in(p).wait()
        last = layer_ref[p] == CAP - 1

        @pl.when(last)
        def _():
            copy_out(p, last_out).start()

        @pl.when(jnp.logical_not(last))
        def _():
            copy_out(p, pair_out).start()

    for p in range(count):
        copy_out(p, pair_out).wait()


def pack(layer_of, dest_of, intensities, cols):
    count, side = intensities.shape[:2]
    smem = pl.BlockSpec(memory_space=pltpu.SMEM)
    hbm = pl.BlockSpec(memory_space=pl.ANY)
    return pl.pallas_call(
        pack_kernel,
        out_shape=[
            jax.ShapeDtypeStruct((cols * (CAP - 1), side, side), jnp.float32),
            jax.ShapeDtypeStruct((cols, side, side), jnp.float32),
        ],
        in_specs=[smem, smem, hbm],
        out_specs=[hbm, hbm],
        scratch_shapes=[
            pltpu.VMEM(intensities.shape, jnp.float32),
            pltpu.SemaphoreType.DMA((count,)),
            pltpu.SemaphoreType.DMA((count,)),
        ],
        compiler_params=pltpu.CompilerParams(vmem_limit_bytes=24 * 2**20),
        cost_estimate=pl.CostEstimate(
            flops=0, bytes_accessed=2 * intensities.size * 4, transcendentals=0
        ),
    )(layer_of, dest_of, intensities)


def mm(first, second):
    return jnp.dot(first, second, preferred_element_type=jnp.float32)


def grad_kernel(
    phase,
    meta_ref,
    main_ref,
    below_ref,
    beside_ref,
    corner_ref,
    illum_ref,
    left_ref,
    right_ref,
    meas_ref,
    *refs,
):
    if phase == 0:
        grad_out, probe_out, *refs = refs
    else:
        grad_in, probe_in, out_main, out_right, out_bottom, out_corner, probe_out, *refs = refs
    (
        ext,
        grad,
        probe,
        meas,
        patch_buf,
        live_list,
        load_sem,
        meas_sem,
        grad_sem,
    ) = refs
    tile = main_ref.shape[1]
    side = illum_ref.shape[1]
    strips = ext.shape[1]
    main_strips = tile // LANES
    slots = meta_ref.shape[1]
    loads = []

    def load(src, dst):
        copy = pltpu.make_async_copy(src, dst, load_sem.at[len(loads)])
        copy.start()
        loads.append(copy)

    for c in range(2):
        for j in range(main_strips):
            lanes = pl.ds(j * LANES, LANES)
            load(main_ref.at[c, :, lanes], ext.at[c, j, pl.ds(0, tile)])
            load(below_ref.at[c, :, lanes], ext.at[c, j, pl.ds(tile, side)])
        for j in range(strips - main_strips):
            lanes = pl.ds(j * LANES, LANES)
            load(beside_ref.at[c, :, lanes], ext.at[c, main_strips + j, pl.ds(0, tile)])
            load(corner_ref.at[c, :, lanes], ext.at[c, main_strips + j, pl.ds(tile, side)])
    if phase == 0:
        grad[...] = jnp.zeros(grad.shape, grad.dtype)
        probe[...] = jnp.zeros(probe.shape, probe.dtype)
    else:
        pre = pltpu.make_async_copy(grad_in, grad, grad_sem)
        pre.start()
        probe[...] = probe_in[...]

    def gather_live(s, n):
        alive = meta_ref[2, s] > 0

        @pl.when(alive)
        def _():
            live_list[n] = s

        return n + alive.astype(jnp.int32)

    total = lax.fori_loop(0, slots, gather_live, jnp.int32(0))

    def fetch(n):
        return pltpu.make_async_copy(meas_ref.at[live_list[n]], meas.at[n % 2], meas_sem.at[n % 2])

    @pl.when(total > 0)
    def _():
        fetch(0).start()

    for copy in loads:
        copy.wait()
    if phase > 0:
        pre.wait()

    lane = lax.broadcasted_iota(jnp.int32, (side, LANES), 1)

    def step(n, carry):
        @pl.when(n + 1 < total)
        def _():
            fetch(n + 1).start()

        s = live_list[n]
        row = meta_ref[0, s]
        col = meta_ref[1, s]
        strip = col // LANES
        shift = col - strip * LANES
        back_shift = (LANES - shift) % LANES
        rows = pl.ds(row, side)
        keep = lane < LANES - shift
        for c in range(2):
            rolled = [pltpu.roll(ext[c, strip + t, rows, :], back_shift, 1) for t in range(3)]
            for t in range(2):
                patch_buf[c, :, pl.ds(t * LANES, LANES)] = jnp.where(keep, rolled[t], rolled[t + 1])
        il_re, il_im = illum_ref[0], illum_ref[1]
        pa_re, pa_im = patch_buf[0], patch_buf[1]
        exit_wave = jnp.concatenate(
            [
                (il_re * pa_re - il_im * pa_im).astype(jnp.bfloat16),
                (il_re * pa_im + il_im * pa_re).astype(jnp.bfloat16),
            ],
            axis=0,
        )
        forward, backward = left_ref[...], right_ref[...]
        mid = mm(forward, exit_wave).astype(jnp.bfloat16)
        wave = mm(jnp.concatenate([mid[:side], mid[side:]], axis=1), backward)
        w_re, w_im = wave[:, :side], wave[:, side:]
        fetch(n).wait()
        measured = meas[n % 2]
        power = jnp.maximum(w_re * w_re + w_im * w_im, 0.25)
        factor = 1.0 - measured * lax.rsqrt(measured * power)
        diff = jnp.concatenate(
            [(w_re * factor).astype(jnp.bfloat16), (w_im * factor).astype(jnp.bfloat16)], axis=0
        )
        mid = mm(backward, diff).astype(jnp.bfloat16)
        back = mm(jnp.concatenate([mid[:side], mid[side:]], axis=1), forward)
        b_re, b_im = back[:, :side], back[:, side:]
        pa_re, pa_im = patch_buf[0], patch_buf[1]
        probe[0] += pa_re * b_re + pa_im * b_im
        probe[1] += pa_re * b_im - pa_im * b_re
        terms = (il_re * b_re + il_im * b_im, il_re * b_im - il_im * b_re)
        early = lane < shift
        for c in range(2):
            first = pltpu.roll(terms[c][:, :LANES], shift, 1)
            second = pltpu.roll(terms[c][:, LANES:], shift, 1)
            grad[c, strip, rows, :] += jnp.where(early, 0.0, first)
            grad[c, strip + 1, rows, :] += jnp.where(early, first, second)
            grad[c, strip + 2, rows, :] += jnp.where(early, second, 0.0)
        return carry

    lax.fori_loop(0, total, step, 0)
    probe_out[...] = probe[...]
    if phase == 0:
        post = pltpu.make_async_copy(grad, grad_out, grad_sem)
        post.start()
        post.wait()
        return
    stores = []

    def store(src, dst):
        copy = pltpu.make_async_copy(src, dst, load_sem.at[len(stores)])
        copy.start()
        stores.append(copy)

    for c in range(2):
        for j in range(strips):
            in_main = j < main_strips
            upper, lower = (out_main, out_bottom) if in_main else (out_right, out_corner)
            lanes = pl.ds((j if in_main else j - main_strips) * LANES, LANES)
            store(grad.at[c, j, pl.ds(0, tile)], upper.at[c, :, lanes])
            store(grad.at[c, j, pl.ds(tile, side)], lower.at[c, :, lanes])
    for copy in stores:
        copy.wait()


def add_chunk(meta, pieces, illumination, tables, measured, so_far):
    main = pieces[0]
    tile, side = main.shape[1], illumination.shape[1]
    strips = (tile + side) // LANES
    grad_shape = (2, strips, tile + side, LANES)
    count = measured.shape[0]
    vmem = pl.BlockSpec(memory_space=pltpu.VMEM)
    smem = pl.BlockSpec(memory_space=pltpu.SMEM)
    hbm = pl.BlockSpec(memory_space=pl.ANY)
    probe_shape = jax.ShapeDtypeStruct((2, side, side), jnp.float32)
    if so_far:
        sizes = [(tile, tile), (tile, side), (side, tile), (side, side)]
        grads = [jax.ShapeDtypeStruct((2,) + size, jnp.float32) for size in sizes]
    else:
        grads = [jax.ShapeDtypeStruct(grad_shape, jnp.float32)]
    return pl.pallas_call(
        functools.partial(grad_kernel, 1 if so_far else 0),
        out_shape=grads + [probe_shape],
        in_specs=[smem, hbm, hbm, hbm, hbm, vmem, vmem, vmem, hbm] + ([hbm, vmem] if so_far else []),
        out_specs=[hbm] * len(grads) + [vmem],
        scratch_shapes=[
            pltpu.VMEM(grad_shape, jnp.float32),
            pltpu.VMEM(grad_shape, jnp.float32),
            pltpu.VMEM((2, side, side), jnp.float32),
            pltpu.VMEM((2, side, side), jnp.float32),
            pltpu.VMEM((2, side, side), jnp.float32),
            pltpu.SMEM((count,), jnp.int32),
            pltpu.SemaphoreType.DMA((4 * strips,)),
            pltpu.SemaphoreType.DMA((2,)),
            pltpu.SemaphoreType.DMA,
        ],
        compiler_params=pltpu.CompilerParams(vmem_limit_bytes=40 * 2**20),
        cost_estimate=pl.CostEstimate(
            flops=count * 16 * 2 * side**3,
            bytes_accessed=count * 4 * side * side + 3 * 8 * (tile + side) ** 2,
            transcendentals=count * side * side,
        ),
    )(meta, *pieces, illumination, *tables, measured, *so_far)


def tail_kernel(
    rows,
    cols,
    right_ref,
    bottom_ref,
    corner_ref,
    probe_ref,
    got_right,
    got_bottom,
    probe_out,
    got_corner,
    right_top,
    part,
    row_sum,
    piece,
    total,
    gathered,
    edge_send,
    edge_recv,
    row_send,
    row_recv,
    col_send,
    col_recv,
):
    r, c = lax.axis_index("row"), lax.axis_index("col")
    side = corner_ref.shape[1]
    below, right = lax.rem(r + 1, rows), lax.rem(c + 1, cols)
    barrier = pltpu.get_barrier_semaphore()
    for o in range(1, rows):
        pl.semaphore_signal(barrier, device_id=(lax.rem(r + o, rows), c), device_id_type=pl.DeviceIdType.MESH)
    for o in range(1, cols):
        pl.semaphore_signal(barrier, device_id=(r, lax.rem(c + o, cols)), device_id_type=pl.DeviceIdType.MESH)
    pl.semaphore_wait(barrier, rows + cols - 2)

    def send(src, dst, send_sem, recv_sem, device):
        copy = pltpu.make_async_remote_copy(
            src_ref=src,
            dst_ref=dst,
            send_sem=send_sem,
            recv_sem=recv_sem,
            device_id=device,
            device_id_type=pl.DeviceIdType.MESH,
        )
        copy.start()
        return copy

    top, rest = pl.ds(0, side), pl.ds(side, right_ref.shape[1] - side)
    to_corner = send(corner_ref, got_corner, edge_send.at[0], edge_recv.at[0], (below, c))
    to_rest = send(
        right_ref.at[:, rest], got_right.at[:, rest], edge_send.at[1], edge_recv.at[1], (r, right)
    )
    first = [
        send(probe_ref.at[lax.rem(r + o, rows)], part.at[o], row_send.at[0, o], row_recv.at[0, o], (lax.rem(r + o, rows), c))
        for o in range(1, rows)
    ]
    to_bottom = send(bottom_ref, got_bottom, edge_send.at[2], edge_recv.at[2], (below, c))
    to_corner.wait()
    right_top[...] = right_ref[:, top, :] + got_corner[...]
    to_top = send(right_top, got_right.at[:, top], edge_send.at[3], edge_recv.at[3], (r, right))

    for copy in first:
        copy.wait()
    summed = probe_ref[r]
    for o in range(1, rows):
        summed = summed + part[o]
    row_sum[...] = summed
    second = [
        send(row_sum.at[lax.rem(c + o, cols)], piece.at[o], col_send.at[0, o], col_recv.at[0, o], (r, lax.rem(c + o, cols)))
        for o in range(1, cols)
    ]
    for copy in second:
        copy.wait()
    whole = row_sum[c]
    for o in range(1, cols):
        whole = whole + piece[o]
    total[...] = whole
    gathered[c] = whole
    third = [
        send(total, gathered.at[c], col_send.at[1, o], col_recv.at[1, o], (r, lax.rem(c + o, cols)))
        for o in range(1, cols)
    ]
    for copy in third:
        copy.wait()
    probe_out[r] = gathered[...]
    fourth = [
        send(gathered, probe_out.at[r], row_send.at[1, o], row_recv.at[1, o], (lax.rem(r + o, rows), c))
        for o in range(1, rows)
    ]
    for copy in fourth:
        copy.wait()
    to_bottom.wait()
    to_rest.wait()
    to_top.wait()


def tail(right, bottom, corner, probe, rows, cols):
    side = corner.shape[1]
    width = probe.size // (rows * cols * 8)
    vmem = pl.BlockSpec(memory_space=pltpu.VMEM)
    dma = pltpu.SemaphoreType.DMA
    split = jax.ShapeDtypeStruct((rows, cols, 8, width), jnp.float32)
    got_right, got_bottom, probe_sum = pl.pallas_call(
        functools.partial(tail_kernel, rows, cols),
        out_shape=[
            jax.ShapeDtypeStruct(right.shape, jnp.float32),
            jax.ShapeDtypeStruct(bottom.shape, jnp.float32),
            split,
        ],
        in_specs=[vmem] * 4,
        out_specs=[vmem] * 3,
        scratch_shapes=[
            pltpu.VMEM((2, side, side), jnp.float32),
            pltpu.VMEM((2, side, side), jnp.float32),
            pltpu.VMEM((rows, cols, 8, width), jnp.float32),
            pltpu.VMEM((cols, 8, width), jnp.float32),
            pltpu.VMEM((cols, 8, width), jnp.float32),
            pltpu.VMEM((8, width), jnp.float32),
            pltpu.VMEM((cols, 8, width), jnp.float32),
            dma((4,)),
            dma((4,)),
            dma((2, rows)),
            dma((2, rows)),
            dma((2, cols)),
            dma((2, cols)),
        ],
        compiler_params=pltpu.CompilerParams(
            collective_id=0, has_side_effects=True, vmem_limit_bytes=32 * 2**20
        ),
    )(right, bottom, corner, probe.reshape(split.shape))
    return got_right, got_bottom, probe_sum.reshape(probe.shape)


def on_device(object_field, illumination, positions, owners, intensities):
    tile = object_field.shape[1]
    side = illumination.shape[1]
    cols = lax.axis_size("col")
    row_count = lax.axis_size("row")
    pos_dev = positions.shape[0]
    band = lax.axis_index("row")
    column = lax.axis_index("col")
    limit_rows = row_count * tile - side
    limit_cols = cols * tile - side

    hits = (owners[:, None] == jnp.arange(cols, dtype=jnp.int32)[None, :]).astype(jnp.int32)
    layer_of = jnp.sum((jnp.cumsum(hits, axis=0) - hits) * hits, axis=1)
    slot_of = owners * CAP + layer_of
    dest_of = jnp.where(layer_of == CAP - 1, owners, owners * (CAP - 1) + layer_of)
    request = jnp.stack([positions[:, 0], positions[:, 1], jnp.ones((pos_dev,), jnp.int32)], axis=1)
    chosen = (slot_of[:, None] == jnp.arange(cols * CAP, dtype=jnp.int32)[None, :]).astype(jnp.int32)
    request_buf = jnp.sum(chosen[:, :, None] * request[:, None, :], axis=0)
    got = lax.all_to_all(request_buf, "col", split_axis=0, concat_axis=0, tiled=True)

    below = passed_along(object_field[:, :side, :], "row", -1)
    beside = passed_along(object_field[:, :, :side], "col", -1)
    corner = passed_along(beside[:, :side, :], "row", -1)
    pieces = (object_field, below, beside, corner)

    pairs, lasts = pack(layer_of, dest_of, intensities, cols)
    pairs, got = lax.optimization_barrier((pairs, got))
    row_at = jnp.minimum(band * tile + got[:, 0], limit_rows) - band * tile
    col_at = jnp.minimum(column * tile + got[:, 1], limit_cols) - column * tile
    meta = jnp.stack([row_at, col_at, got[:, 2]]).reshape(3, cols, CAP)

    t_re, t_im = dft_tables(side)
    tables = (
        jnp.block([[t_re, -t_im], [t_im, t_re]]),
        jnp.block([[t_re, t_im], [-t_im, t_re]]),
    )

    pairs = lax.all_to_all(pairs, "col", split_axis=0, concat_axis=0, tiled=True)
    lasts, pairs = lax.optimization_barrier((lasts, pairs))
    lasts = lax.all_to_all(lasts, "col", split_axis=0, concat_axis=0, tiled=True)
    so_far = add_chunk(
        meta[:, :, : CAP - 1].reshape(3, -1), pieces, illumination, tables, pairs, ()
    )
    main, right, bottom, corner, probe = add_chunk(
        meta[:, :, CAP - 1], pieces, illumination, tables, lasts, so_far
    )
    from_left, from_above, probe_total = tail(right, bottom, corner, probe, row_count, cols)
    probe_grad = probe_total / math.sqrt(pos_dev * row_count * cols)
    object_grad = main.at[:, :, :side].add(from_left).at[:, :side, :].add(from_above)
    return (object_grad, probe_grad)


def solution(mesh):
    return jax.shard_map(
        on_device,
        mesh=mesh,
        in_specs=(
            P(None, "row", "col"),
            P(),
            P(("row", "col"), None),
            P(("row", "col")),
            P(("row", "col"), None, None),
        ),
        out_specs=(P(None, "row", "col"), P()),
        check_vma=False,
    )
```

```python
import functools
import math

import jax
import jax.numpy as jnp
from jax import lax
from jax.experimental import pallas as pl
from jax.experimental.pallas import tpu as pltpu
from jax.sharding import PartitionSpec as P

CAP = 3
LANES = 128
GROUP = 2


def passed_along(value, axis, steps):
    count = lax.axis_size(axis)
    leading, last = (max(0, -steps), min(count, count - steps))
    return lax.ppermute(value, axis, [(source, source + steps) for source in range(leading, last)])


def dft_tables(length):
    grid_ids = jnp.arange(length, dtype=jnp.int32)
    phase_ids = grid_ids[:, None] * grid_ids[None, :] % length
    angles = phase_ids.astype(jnp.float32) * (2.0 * math.pi / length)
    scale_factor = 1.0 / math.sqrt(length)
    return (
        (jnp.cos(angles) * scale_factor).astype(jnp.bfloat16),
        (-jnp.sin(angles) * scale_factor).astype(jnp.bfloat16),
    )


def pack_kernel(layer_ref, dest_ref, src_ref, pair_out, last_out, held, in_sem, out_sem):
    count = src_ref.shape[0]

    def copy_in(p):
        return pltpu.make_async_copy(src_ref.at[p], held.at[p], in_sem.at[p])

    def copy_out(p, out):
        return pltpu.make_async_copy(held.at[p], out.at[dest_ref[p]], out_sem.at[p])

    for p in range(count):
        copy_in(p).start()
    for p in range(count):
        copy_in(p).wait()
        last = layer_ref[p] == CAP - 1

        @pl.when(last)
        def _():
            copy_out(p, last_out).start()

        @pl.when(jnp.logical_not(last))
        def _():
            copy_out(p, pair_out).start()

    for p in range(count):
        copy_out(p, pair_out).wait()


def pack(layer_of, dest_of, intensities, cols):
    count, side = intensities.shape[:2]
    smem = pl.BlockSpec(memory_space=pltpu.SMEM)
    hbm = pl.BlockSpec(memory_space=pl.ANY)
    return pl.pallas_call(
        pack_kernel,
        out_shape=[
            jax.ShapeDtypeStruct((cols * (CAP - 1), side, side), jnp.float32),
            jax.ShapeDtypeStruct((cols, side, side), jnp.float32),
        ],
        in_specs=[smem, smem, hbm],
        out_specs=[hbm, hbm],
        scratch_shapes=[
            pltpu.VMEM(intensities.shape, jnp.float32),
            pltpu.SemaphoreType.DMA((count,)),
            pltpu.SemaphoreType.DMA((count,)),
        ],
        compiler_params=pltpu.CompilerParams(vmem_limit_bytes=24 * 2**20),
        cost_estimate=pl.CostEstimate(
            flops=0, bytes_accessed=2 * intensities.size * 4, transcendentals=0
        ),
    )(layer_of, dest_of, intensities)


def mm(first, second):
    return jnp.dot(first, second, preferred_element_type=jnp.float32)


def tiles_of(side):
    return [
        (c, pl.ds(i, 8), pl.ds(j, LANES))
        for c in range(2)
        for i in range(0, side, 8)
        for j in range(0, side, LANES)
    ]


def grad_kernel(
    phase,
    meta_ref,
    next_ref,
    main_ref,
    below_ref,
    beside_ref,
    corner_ref,
    illum_ref,
    left_ref,
    right_ref,
    meas_ref,
    *refs,
):
    if phase == 0:
        grad_out, probe_out, waves_out, *refs = refs
    else:
        (
            grad_in,
            probe_in,
            waves_in,
            out_main,
            out_right,
            out_bottom,
            out_corner,
            probe_out,
            *refs,
        ) = refs
    ext, grad, probe, meas, waves, *refs = refs
    patches, (live_list, load_sem, meas_sem, wave_sem, grad_sem) = refs[:GROUP], refs[GROUP:]
    tile = main_ref.shape[1]
    side = illum_ref.shape[1]
    strips = ext.shape[1]
    main_strips = tile // LANES
    slots = meta_ref.shape[1]
    loads = []

    def load(src, dst):
        copy = pltpu.make_async_copy(src, dst, load_sem.at[len(loads)])
        copy.start()
        loads.append(copy)

    for c in range(2):
        for j in range(main_strips):
            lanes = pl.ds(j * LANES, LANES)
            load(main_ref.at[c, :, lanes], ext.at[c, j, pl.ds(0, tile)])
            load(below_ref.at[c, :, lanes], ext.at[c, j, pl.ds(tile, side)])
        for j in range(strips - main_strips):
            lanes = pl.ds(j * LANES, LANES)
            load(beside_ref.at[c, :, lanes], ext.at[c, main_strips + j, pl.ds(0, tile)])
            load(corner_ref.at[c, :, lanes], ext.at[c, main_strips + j, pl.ds(tile, side)])
    if phase == 0:
        grad[...] = jnp.zeros(grad.shape, grad.dtype)
        probe[...] = jnp.zeros(probe.shape, probe.dtype)
    else:
        pre = pltpu.make_async_copy(grad_in, grad, grad_sem)
        pre.start()
        probe[...] = probe_in[...]

    def list_live(layer_ref):
        def gather_live(s, n):
            alive = layer_ref[2, s] > 0

            @pl.when(alive)
            def _():
                live_list[n] = s

            return n + alive.astype(jnp.int32)

        return lax.fori_loop(0, layer_ref.shape[1], gather_live, jnp.int32(0))

    total = list_live(meta_ref)

    def fetch(n):
        slot = n % (2 * GROUP)
        at = jnp.minimum(n, total - 1)
        place = live_list[at]
        copies = [pltpu.make_async_copy(meas_ref.at[place], meas.at[slot], meas_sem.at[slot])]
        if phase > 0:
            copies.append(
                pltpu.make_async_copy(waves_in.at[at], waves.at[slot], wave_sem.at[slot])
            )
        return copies

    @pl.when(total > 0)
    def _():
        for i in range(GROUP):
            for copy in fetch(i):
                copy.start()

    for copy in loads:
        copy.wait()
    if phase > 0:
        pre.wait()

    lane = lax.broadcasted_iota(jnp.int32, (side, LANES), 1)
    each = range(GROUP)
    il_re, il_im = illum_ref[0], illum_ref[1]

    def places_of(layer_ref, base, count):
        places = []
        for i in each:
            s = live_list[jnp.minimum(base + i, count - 1)]
            col = layer_ref[1, s]
            strip = col // LANES
            places.append((pl.ds(layer_ref[0, s], side), strip, col - strip * LANES))
        return places

    def patch_of(place):
        rows, strip, shift = place
        back_shift = (LANES - shift) % LANES
        keep = lane < LANES - shift
        patch = []
        for c in range(2):
            rolled = [pltpu.roll(ext[c, strip + t, rows, :], back_shift, 1) for t in range(3)]
            whole = [jnp.where(keep, rolled[t], rolled[t + 1]) for t in range(2)]
            patch.append(jnp.concatenate(whole, axis=1))
        return patch

    def exit_of(patch):
        pa_re, pa_im = patch
        parts = [il_re * pa_re - il_im * pa_im, il_re * pa_im + il_im * pa_re]
        return jnp.concatenate([part.astype(jnp.bfloat16) for part in parts], axis=0)

    def halves(stage):
        return jnp.concatenate([stage[:side], stage[side:]], axis=1)

    def step(g, carry):
        base = g * GROUP

        @pl.when((g + 1) * GROUP < total)
        def _():
            for i in each:
                for copy in fetch(base + GROUP + i):
                    copy.start()

        for i in each:
            for copy in fetch(base + i):
                copy.wait()
        places = places_of(meta_ref, base, total)
        weights = [jnp.where(base + i < total, 1.0, 0.0) for i in each]
        forward, backward = left_ref[...], right_ref[...]

        def residual(i, wave):
            w_re, w_im = wave[:, :side], wave[:, side:]
            measured = meas[(base + i) % (2 * GROUP)]
            power = jnp.maximum(w_re * w_re + w_im * w_im, 0.25)
            factor = 1.0 - measured * lax.rsqrt(measured * power)
            if i > 0:
                factor = factor * weights[i]
            parts = [(w_re * factor).astype(jnp.bfloat16), (w_im * factor).astype(jnp.bfloat16)]
            return jnp.concatenate(parts, axis=0)

        def leave(i, back):
            rows, strip, shift = places[i]
            b_re, b_im = back[:, :side], back[:, side:]
            if phase == 0:
                pa_re, pa_im = patches[i][0], patches[i][1]
            else:
                pa_re, pa_im = patch_of(places[i])
            terms = (il_re * b_re + il_im * b_im, il_re * b_im - il_im * b_re)
            early = lane < shift
            for c in range(2):
                one = pltpu.roll(terms[c][:, :LANES], shift, 1)
                two = pltpu.roll(terms[c][:, LANES:], shift, 1)
                grad[c, strip, rows, :] += jnp.where(early, 0.0, one)
                grad[c, strip + 1, rows, :] += jnp.where(early, one, two)
                grad[c, strip + 2, rows, :] += jnp.where(early, two, 0.0)
            return pa_re * b_re + pa_im * b_im, pa_re * b_im - pa_im * b_re

        if phase == 0:
            exits = []
            for i in each:
                patch = patch_of(places[i])
                patches[i][0], patches[i][1] = patch
                exits.append(exit_of(patch))
            mids = [mm(forward, exits[i]).astype(jnp.bfloat16) for i in each]
            diffs = [residual(i, mm(halves(mids[i]), backward)) for i in each]
        else:
            diffs = [residual(i, waves[(base + i) % (2 * GROUP)]) for i in each]
        mids = [mm(backward, diffs[i]).astype(jnp.bfloat16) for i in each]
        terms = [leave(i, mm(halves(mids[i]), forward)) for i in each]
        probe[0] += sum(term[0] for term in terms)
        probe[1] += sum(term[1] for term in terms)
        return carry

    lax.fori_loop(0, (total + GROUP - 1) // GROUP, step, 0)
    if phase == 0:
        post = pltpu.make_async_copy(grad, grad_out, grad_sem)
        post.start()
        after = list_live(next_ref)
        rounds = (after + GROUP - 1) // GROUP

        def keep_wave(n):
            return pltpu.make_async_copy(waves.at[n], waves_out.at[n], wave_sem.at[n])

        def ready(g, carry):
            base = g * GROUP
            places = places_of(next_ref, base, after)
            forward, backward = left_ref[...], right_ref[...]
            exits = [exit_of(patch_of(places[i])) for i in each]
            mids = [mm(forward, exits[i]).astype(jnp.bfloat16) for i in each]
            for i in each:
                waves[base + i] = mm(halves(mids[i]), backward)
            for i in each:
                keep_wave(base + i).start()
            return carry

        lax.fori_loop(0, rounds, ready, 0)
        probe_out[...] = probe[...]

        def kept(n, carry):
            keep_wave(n).wait()
            return carry

        lax.fori_loop(0, rounds * GROUP, kept, 0)
        post.wait()
        return
    stores = []

    def store(src, dst):
        copy = pltpu.make_async_copy(src, dst, load_sem.at[len(stores)])
        copy.start()
        stores.append(copy)

    for c in range(2):
        for j in range(strips):
            in_main = j < main_strips
            upper, lower = (out_main, out_bottom) if in_main else (out_right, out_corner)
            lanes = pl.ds((j if in_main else j - main_strips) * LANES, LANES)
            store(grad.at[c, j, pl.ds(0, tile)], upper.at[c, :, lanes])
            store(grad.at[c, j, pl.ds(tile, side)], lower.at[c, :, lanes])
    for t, (c, down, across) in enumerate(tiles_of(side)):
        probe_out[t] = probe[c, down, across]
    for copy in stores:
        copy.wait()


def add_chunk(meta, next_meta, pieces, illumination, tables, measured, so_far):
    main = pieces[0]
    tile, side = main.shape[1], illumination.shape[1]
    strips = (tile + side) // LANES
    grad_shape = (2, strips, tile + side, LANES)
    last_count = next_meta.shape[1]
    vmem = pl.BlockSpec(memory_space=pltpu.VMEM)
    smem = pl.BlockSpec(memory_space=pltpu.SMEM)
    hbm = pl.BlockSpec(memory_space=pltpu.HBM)
    both = (2, side, side)
    if so_far:
        sizes = [(2, tile, tile), (2, tile, side), (2, side, tile), both]
        sizes.append((2 * side * side // (8 * LANES), 8, LANES))
        out_specs = [hbm] * 4 + [vmem]
        held = 2 * GROUP
    else:
        sizes = [grad_shape, both, (last_count, side, 2 * side)]
        out_specs = [hbm, vmem, hbm]
        held = last_count
    count = measured.shape[0]
    return pl.pallas_call(
        functools.partial(grad_kernel, 1 if so_far else 0),
        out_shape=[jax.ShapeDtypeStruct(size, jnp.float32) for size in sizes],
        in_specs=[smem] * 2
        + [hbm] * 4
        + [vmem] * 3
        + [hbm]
        + ([hbm, vmem, hbm] if so_far else []),
        out_specs=out_specs,
        scratch_shapes=[
            pltpu.VMEM(grad_shape, jnp.float32),
            pltpu.VMEM(grad_shape, jnp.float32),
            pltpu.VMEM(both, jnp.float32),
            pltpu.VMEM((2 * GROUP, side, side), jnp.float32),
            pltpu.VMEM((held, side, 2 * side), jnp.float32),
            *[pltpu.VMEM(both, jnp.float32) for _ in range(GROUP)],
            pltpu.SMEM((max(count, last_count),), jnp.int32),
            pltpu.SemaphoreType.DMA((4 * strips,)),
            pltpu.SemaphoreType.DMA((2 * GROUP,)),
            pltpu.SemaphoreType.DMA((held,)),
            pltpu.SemaphoreType.DMA,
        ],
        compiler_params=pltpu.CompilerParams(vmem_limit_bytes=48 * 2**20),
        cost_estimate=pl.CostEstimate(
            flops=count * 16 * 2 * side**3,
            bytes_accessed=count * 4 * side * side + 3 * 8 * (tile + side) ** 2,
            transcendentals=count * side * side,
        ),
    )(meta, next_meta, *pieces, illumination, *tables, measured, *so_far)


def tail_kernel(
    rows,
    cols,
    scale,
    right_ref,
    bottom_ref,
    corner_ref,
    probe_ref,
    got_right,
    got_bottom,
    probe_out,
    got_corner,
    right_top,
    part,
    row_sum,
    piece,
    total,
    gathered,
    whole_probe,
    top_sem,
    edge_send,
    edge_recv,
    row_send,
    row_recv,
    col_send,
    col_recv,
):
    r, c = lax.axis_index("row"), lax.axis_index("col")
    side = corner_ref.shape[1]
    below, right = lax.rem(r + 1, rows), lax.rem(c + 1, cols)
    top, rest = pl.ds(0, side), pl.ds(side, right_ref.shape[1] - side)
    top_copy = pltpu.make_async_copy(right_ref.at[:, top], right_top, top_sem)
    top_copy.start()
    barrier = pltpu.get_barrier_semaphore()
    for o in range(1, rows):
        pl.semaphore_signal(
            barrier, device_id=(lax.rem(r + o, rows), c), device_id_type=pl.DeviceIdType.MESH
        )
    for o in range(1, cols):
        pl.semaphore_signal(
            barrier, device_id=(r, lax.rem(c + o, cols)), device_id_type=pl.DeviceIdType.MESH
        )
    top_copy.wait()
    pl.semaphore_wait(barrier, rows + cols - 2)

    def send(src, dst, send_sem, recv_sem, device):
        copy = pltpu.make_async_remote_copy(
            src_ref=src,
            dst_ref=dst,
            send_sem=send_sem,
            recv_sem=recv_sem,
            device_id=device,
            device_id_type=pl.DeviceIdType.MESH,
        )
        copy.start()
        return copy

    to_corner = send(corner_ref, got_corner, edge_send.at[0], edge_recv.at[0], (below, c))
    to_rest = send(
        right_ref.at[:, rest], got_right.at[:, rest], edge_send.at[1], edge_recv.at[1], (r, right)
    )
    first = [
        send(probe_ref.at[lax.rem(r + o, rows)], part.at[o], row_send.at[0, o], row_recv.at[0, o], (lax.rem(r + o, rows), c))
        for o in range(1, rows)
    ]
    to_corner.wait()
    right_top[...] += got_corner[...]
    to_top = send(right_top, got_right.at[:, top], edge_send.at[3], edge_recv.at[3], (r, right))

    for copy in first:
        copy.wait()
    to_bottom = send(bottom_ref, got_bottom, edge_send.at[2], edge_recv.at[2], (below, c))
    summed = probe_ref[r]
    for o in range(1, rows):
        summed = summed + part[o]
    row_sum[...] = summed
    second = [
        send(row_sum.at[lax.rem(c + o, cols)], piece.at[o], col_send.at[0, o], col_recv.at[0, o], (r, lax.rem(c + o, cols)))
        for o in range(1, cols)
    ]
    for copy in second:
        copy.wait()
    whole = row_sum[c]
    for o in range(1, cols):
        whole = whole + piece[o]
    total[...] = whole
    gathered[c] = whole
    third = [
        send(total, gathered.at[c], col_send.at[1, o], col_recv.at[1, o], (r, lax.rem(c + o, cols)))
        for o in range(1, cols)
    ]
    for copy in third:
        copy.wait()
    whole_probe[r] = gathered[...]
    fourth = [
        send(gathered, whole_probe.at[r], row_send.at[1, o], row_recv.at[1, o], (lax.rem(r + o, rows), c))
        for o in range(1, rows)
    ]
    for copy in fourth:
        copy.wait()
    for t, (part_at, down, across) in enumerate(tiles_of(side)):
        probe_out[part_at, down, across] = whole_probe[t // cols, t % cols] * scale
    to_bottom.wait()
    to_rest.wait()
    to_top.wait()


def tail(right, bottom, corner, probe, rows, cols, scale):
    side = corner.shape[1]
    share = probe.shape[0] // (rows * cols) * 8
    vmem = pl.BlockSpec(memory_space=pltpu.VMEM)
    hbm = pl.BlockSpec(memory_space=pltpu.HBM)
    dma = pltpu.SemaphoreType.DMA
    split = (rows, cols, share, LANES)
    both = (2, side, side)
    return pl.pallas_call(
        functools.partial(tail_kernel, rows, cols, scale),
        out_shape=[
            jax.ShapeDtypeStruct(right.shape, jnp.float32),
            jax.ShapeDtypeStruct(bottom.shape, jnp.float32),
            jax.ShapeDtypeStruct(both, jnp.float32),
        ],
        in_specs=[hbm] * 3 + [vmem],
        out_specs=[vmem] * 3,
        scratch_shapes=[
            pltpu.VMEM(both, jnp.float32),
            pltpu.VMEM(both, jnp.float32),
            pltpu.VMEM(split, jnp.float32),
            pltpu.VMEM(split[1:], jnp.float32),
            pltpu.VMEM(split[1:], jnp.float32),
            pltpu.VMEM(split[2:], jnp.float32),
            pltpu.VMEM(split[1:], jnp.float32),
            pltpu.VMEM(split, jnp.float32),
            dma,
            dma((4,)),
            dma((4,)),
            dma((2, rows)),
            dma((2, rows)),
            dma((2, cols)),
            dma((2, cols)),
        ],
        compiler_params=pltpu.CompilerParams(
            collective_id=0, has_side_effects=True, vmem_limit_bytes=32 * 2**20
        ),
    )(right, bottom, corner, probe.reshape(split))


def on_device(object_field, illumination, positions, owners, intensities):
    tile = object_field.shape[1]
    side = illumination.shape[1]
    cols = lax.axis_size("col")
    row_count = lax.axis_size("row")
    pos_dev = positions.shape[0]
    band = lax.axis_index("row")
    column = lax.axis_index("col")
    limit_rows = row_count * tile - side
    limit_cols = cols * tile - side

    hits = (owners[:, None] == jnp.arange(cols, dtype=jnp.int32)[None, :]).astype(jnp.int32)
    layer_of = jnp.sum((jnp.cumsum(hits, axis=0) - hits) * hits, axis=1)
    slot_of = owners * CAP + layer_of
    dest_of = jnp.where(layer_of == CAP - 1, owners, owners * (CAP - 1) + layer_of)
    request = jnp.stack([positions[:, 0], positions[:, 1], jnp.ones((pos_dev,), jnp.int32)], axis=1)
    chosen = (slot_of[:, None] == jnp.arange(cols * CAP, dtype=jnp.int32)[None, :]).astype(jnp.int32)
    request_buf = jnp.sum(chosen[:, :, None] * request[:, None, :], axis=0)
    got = lax.all_to_all(request_buf, "col", split_axis=0, concat_axis=0, tiled=True)

    below = passed_along(object_field[:, :side, :], "row", -1)
    beside = passed_along(object_field[:, :, :side], "col", -1)
    corner = passed_along(beside[:, :side, :], "row", -1)
    pieces = (object_field, below, beside, corner)

    pairs, lasts = pack(layer_of, dest_of, intensities, cols)
    pairs, got, pieces = lax.optimization_barrier((pairs, got, pieces))
    row_at = jnp.minimum(band * tile + got[:, 0], limit_rows) - band * tile
    col_at = jnp.minimum(column * tile + got[:, 1], limit_cols) - column * tile
    meta = jnp.stack([row_at, col_at, got[:, 2]]).reshape(3, cols, CAP)

    t_re, t_im = dft_tables(side)
    tables = (
        jnp.block([[t_re, -t_im], [t_im, t_re]]),
        jnp.block([[t_re, t_im], [-t_im, t_re]]),
    )

    pairs = lax.all_to_all(pairs, "col", split_axis=0, concat_axis=0, tiled=True)
    lasts, pairs = lax.optimization_barrier((lasts, pairs))
    lasts = lax.all_to_all(lasts, "col", split_axis=0, concat_axis=0, tiled=True)
    last_meta = meta[:, :, CAP - 1]
    so_far = add_chunk(
        meta[:, :, : CAP - 1].reshape(3, -1), last_meta, pieces, illumination, tables, pairs, ()
    )
    main, right, bottom, corner, probe = add_chunk(
        last_meta, last_meta, pieces, illumination, tables, lasts, so_far
    )
    scale = 1.0 / math.sqrt(pos_dev * row_count * cols)
    from_left, from_above, probe_grad = tail(
        right, bottom, corner, probe, row_count, cols, scale
    )
    past = tile - side
    object_grad = (
        main
        + jnp.pad(from_left, ((0, 0), (0, 0), (0, past)))
        + jnp.pad(from_above, ((0, 0), (0, past), (0, 0)))
    )
    return (object_grad, probe_grad)


def solution(mesh):
    return jax.shard_map(
        on_device,
        mesh=mesh,
        in_specs=(
            P(None, "row", "col"),
            P(),
            P(("row", "col"), None),
            P(("row", "col")),
            P(("row", "col"), None, None),
        ),
        out_specs=(P(None, "row", "col"), P()),
        check_vma=False,
    )
```

```python
import functools
import math

import jax
import jax.numpy as jnp
from jax import lax
from jax.experimental import pallas as pl
from jax.experimental.pallas import tpu as pltpu
from jax.sharding import PartitionSpec as P

CAP = 3
LANES = 128
ASK_ROWS = 8
GROUP = 2


def passed_along(value, axis, steps):
    count = lax.axis_size(axis)
    leading, last = (max(0, -steps), min(count, count - steps))
    return lax.ppermute(value, axis, [(source, source + steps) for source in range(leading, last)])


def dft_tables(length):
    grid_ids = jnp.arange(length, dtype=jnp.int32)
    phase_ids = grid_ids[:, None] * grid_ids[None, :] % length
    angles = phase_ids.astype(jnp.float32) * (2.0 * math.pi / length)
    scale_factor = 1.0 / math.sqrt(length)
    return (
        (jnp.cos(angles) * scale_factor).astype(jnp.bfloat16),
        (-jnp.sin(angles) * scale_factor).astype(jnp.bfloat16),
    )


def pack_kernel(layer_ref, owner_ref, ask_ref, src_ref, pair_out, last_out, held, in_sem, out_sem):
    count, side = src_ref.shape[:2]
    asked = pltpu.make_async_copy(
        ask_ref, pair_out.at[:, pl.ds((CAP - 1) * side, ASK_ROWS)], out_sem.at[count]
    )
    asked.start()

    def copy_in(p):
        return pltpu.make_async_copy(src_ref.at[p], held.at[p], in_sem.at[p])

    def copy_pair(p):
        rows = pl.ds(pl.multiple_of(layer_ref[p] * side, side), side)
        return pltpu.make_async_copy(held.at[p], pair_out.at[owner_ref[p], rows], out_sem.at[p])

    def copy_last(p):
        return pltpu.make_async_copy(held.at[p], last_out.at[owner_ref[p]], out_sem.at[p])

    for p in range(count):
        copy_in(p).start()
    for p in range(count):
        copy_in(p).wait()
        last = layer_ref[p] == CAP - 1

        @pl.when(last)
        def _():
            copy_last(p).start()

        @pl.when(jnp.logical_not(last))
        def _():
            copy_pair(p).start()

    for p in range(count):
        copy_last(p).wait()
    asked.wait()


def pack(layer_of, owners, asks, intensities):
    count, side = intensities.shape[:2]
    cols = asks.shape[0]
    smem = pl.BlockSpec(memory_space=pltpu.SMEM)
    hbm = pl.BlockSpec(memory_space=pltpu.HBM)
    return pl.pallas_call(
        pack_kernel,
        out_shape=[
            jax.ShapeDtypeStruct((cols, (CAP - 1) * side + ASK_ROWS, side), jnp.float32),
            jax.ShapeDtypeStruct((cols, side, side), jnp.float32),
        ],
        in_specs=[smem, smem, hbm, hbm],
        out_specs=[hbm, hbm],
        scratch_shapes=[
            pltpu.VMEM(intensities.shape, jnp.float32),
            pltpu.SemaphoreType.DMA((count,)),
            pltpu.SemaphoreType.DMA((count + 1,)),
        ],
        compiler_params=pltpu.CompilerParams(vmem_limit_bytes=24 * 2**20),
        cost_estimate=pl.CostEstimate(
            flops=0, bytes_accessed=2 * intensities.size * 4, transcendentals=0
        ),
    )(layer_of, owners, asks, intensities)


def dot(first, second):
    return jnp.dot(first, second, preferred_element_type=jnp.float32)


def mm(first, second):
    if first.shape[0] == first.shape[1]:
        half = first.shape[0] // 2
        return jnp.concatenate([dot(first[:half], second), dot(first[half:], second)], axis=0)
    half = second.shape[1] // 2
    return jnp.concatenate([dot(first, second[:, :half]), dot(first, second[:, half:])], axis=1)


def tiles_of(side):
    return [
        (c, pl.ds(i, 8), pl.ds(j, LANES))
        for c in range(2)
        for i in range(0, side, 8)
        for j in range(0, side, LANES)
    ]


def grad_kernel(
    phase,
    meta_ref,
    next_ref,
    main_ref,
    below_ref,
    beside_ref,
    corner_ref,
    left_in,
    right_in,
    meas_ref,
    *refs,
):
    if phase == 0:
        illum_in, grad_out, waves_out, *refs = refs
    else:
        (
            grad_in,
            waves_in,
            out_main,
            out_right,
            out_bottom,
            out_corner,
            probe_out,
            *refs,
        ) = refs
    ext, grad, probe, illum_ref, left_ref, right_ref, meas, waves, *refs = refs
    patches, (live_list, load_sem, meas_sem, wave_sem) = refs[:GROUP], refs[GROUP:]
    tile = main_ref.shape[1]
    side = illum_ref.shape[1]
    strips = ext.shape[1]
    main_strips = tile // LANES
    slots = meta_ref.shape[1]
    loads = []

    def load(src, dst):
        copy = pltpu.make_async_copy(src, dst, load_sem.at[len(loads)])
        copy.start()
        loads.append(copy)

    both_strips = [(c, j) for c in range(2) for j in range(side // LANES)]
    held_at = [(c, pl.ds(j * side, side)) for c, j in both_strips]
    if phase == 0:
        load(illum_in, illum_ref)
    load(left_in, left_ref)
    load(right_in, right_ref)
    for c in range(2):
        for j in range(main_strips):
            lanes = pl.ds(j * LANES, LANES)
            load(main_ref.at[c, :, lanes], ext.at[c, j, pl.ds(0, tile)])
            load(below_ref.at[c, :, lanes], ext.at[c, j, pl.ds(tile, side)])
        for j in range(strips - main_strips):
            lanes = pl.ds(j * LANES, LANES)
            load(beside_ref.at[c, :, lanes], ext.at[c, main_strips + j, pl.ds(0, tile)])
            load(corner_ref.at[c, :, lanes], ext.at[c, main_strips + j, pl.ds(tile, side)])
    if phase == 0:
        grad[...] = jnp.zeros(grad.shape, grad.dtype)
        probe[...] = jnp.zeros(probe.shape, probe.dtype)
    else:
        for (c, j), (at, rows) in zip(both_strips, held_at):
            lanes = pl.ds(j * LANES, LANES)
            load(grad_in.at[2 * strips + at, rows], probe.at[c, :, lanes])
            load(grad_in.at[2 * strips + 2 + at, rows], illum_ref.at[c, :, lanes])
        for c in range(2):
            load(grad_in.at[pl.ds(c * strips, strips)], grad.at[c])

    def list_live(layer_ref):
        def gather_live(s, n):
            alive = layer_ref[2, s] > 0

            @pl.when(alive)
            def _():
                live_list[n] = s

            return n + alive.astype(jnp.int32)

        return lax.fori_loop(0, layer_ref.shape[1], gather_live, jnp.int32(0))

    total = list_live(meta_ref)

    def fetch(n):
        slot = n % (2 * GROUP)
        at = jnp.minimum(n, total - 1)
        place = live_list[at]
        if phase == 0:
            source = place // (CAP - 1)
            layer = place - source * (CAP - 1)
            found = meas_ref.at[source, pl.ds(pl.multiple_of(layer * side, side), side)]
        else:
            found = meas_ref.at[place]
        copies = [pltpu.make_async_copy(found, meas.at[slot], meas_sem.at[slot])]
        if phase > 0:
            copies.append(
                pltpu.make_async_copy(waves_in.at[at], waves.at[slot], wave_sem.at[slot])
            )
        return copies

    @pl.when(total > 0)
    def _():
        for i in range(GROUP):
            for copy in fetch(i):
                copy.start()

    for copy in loads:
        copy.wait()

    lane = lax.broadcasted_iota(jnp.int32, (side, LANES), 1)
    each = range(GROUP)
    il_re, il_im = illum_ref[0], illum_ref[1]

    def places_of(layer_ref, base, count):
        places = []
        for i in each:
            s = live_list[jnp.minimum(base + i, count - 1)]
            col = layer_ref[1, s]
            strip = col // LANES
            places.append((pl.ds(layer_ref[0, s], side), strip, col - strip * LANES))
        return places

    def patch_of(place):
        rows, strip, shift = place
        back_shift = (LANES - shift) % LANES
        keep = lane < LANES - shift
        patch = []
        for c in range(2):
            rolled = [pltpu.roll(ext[c, strip + t, rows, :], back_shift, 1) for t in range(3)]
            whole = [jnp.where(keep, rolled[t], rolled[t + 1]) for t in range(2)]
            patch.append(jnp.concatenate(whole, axis=1))
        return patch

    def exit_of(patch):
        pa_re, pa_im = patch
        parts = [il_re * pa_re - il_im * pa_im, il_re * pa_im + il_im * pa_re]
        return jnp.concatenate([part.astype(jnp.bfloat16) for part in parts], axis=0)

    def halves(stage):
        return jnp.concatenate([stage[:side], stage[side:]], axis=1)

    def step(g, carry):
        base = g * GROUP

        @pl.when((g + 1) * GROUP < total)
        def _():
            for i in each:
                for copy in fetch(base + GROUP + i):
                    copy.start()

        for i in each:
            for copy in fetch(base + i):
                copy.wait()
        places = places_of(meta_ref, base, total)
        weights = [jnp.where(base + i < total, 1.0, 0.0) for i in each]
        forward, backward = left_ref[...], right_ref[...]

        def residual(i, wave):
            w_re, w_im = wave[:, :side], wave[:, side:]
            measured = meas[(base + i) % (2 * GROUP)]
            power = jnp.maximum(w_re * w_re + w_im * w_im, 0.25)
            factor = 1.0 - measured * lax.rsqrt(measured * power)
            if i > 0:
                factor = factor * weights[i]
            parts = [(w_re * factor).astype(jnp.bfloat16), (w_im * factor).astype(jnp.bfloat16)]
            return jnp.concatenate(parts, axis=0)

        def leave(i, back):
            rows, strip, shift = places[i]
            b_re, b_im = back[:, :side], back[:, side:]
            if phase == 0:
                pa_re, pa_im = patches[i][0], patches[i][1]
            else:
                pa_re, pa_im = patch_of(places[i])
            terms = (il_re * b_re + il_im * b_im, il_re * b_im - il_im * b_re)
            early = lane < shift
            for c in range(2):
                one = pltpu.roll(terms[c][:, :LANES], shift, 1)
                two = pltpu.roll(terms[c][:, LANES:], shift, 1)
                grad[c, strip, rows, :] += jnp.where(early, 0.0, one)
                grad[c, strip + 1, rows, :] += jnp.where(early, one, two)
                grad[c, strip + 2, rows, :] += jnp.where(early, two, 0.0)
            return pa_re * b_re + pa_im * b_im, pa_re * b_im - pa_im * b_re

        if phase == 0:
            exits = []
            for i in each:
                patch = patch_of(places[i])
                patches[i][0], patches[i][1] = patch
                exits.append(exit_of(patch))
            mids = [mm(forward, exits[i]).astype(jnp.bfloat16) for i in each]
            diffs = [residual(i, mm(halves(mids[i]), backward)) for i in each]
        else:
            diffs = [residual(i, waves[(base + i) % (2 * GROUP)]) for i in each]
        mids = [mm(backward, diffs[i]).astype(jnp.bfloat16) for i in each]
        terms = [leave(i, mm(halves(mids[i]), forward)) for i in each]
        probe[0] += sum(term[0] for term in terms)
        probe[1] += sum(term[1] for term in terms)
        return carry

    lax.fori_loop(0, (total + GROUP - 1) // GROUP, step, 0)
    if phase == 0:
        posts = []

        def post(src, dst):
            copy = pltpu.make_async_copy(src, dst, load_sem.at[len(posts)])
            copy.start()
            posts.append(copy)

        for c in range(2):
            post(grad.at[c], grad_out.at[pl.ds(c * strips, strips)])
        for (c, j), (at, rows) in zip(both_strips, held_at):
            lanes = pl.ds(j * LANES, LANES)
            post(probe.at[c, :, lanes], grad_out.at[2 * strips + at, rows])
            post(illum_ref.at[c, :, lanes], grad_out.at[2 * strips + 2 + at, rows])
        after = list_live(next_ref)
        rounds = (after + GROUP - 1) // GROUP

        def keep_wave(n):
            return pltpu.make_async_copy(waves.at[n], waves_out.at[n], wave_sem.at[n])

        def ready(g, carry):
            base = g * GROUP
            places = places_of(next_ref, base, after)
            forward, backward = left_ref[...], right_ref[...]
            exits = [exit_of(patch_of(places[i])) for i in each]
            mids = [mm(forward, exits[i]).astype(jnp.bfloat16) for i in each]
            for i in each:
                waves[base + i] = mm(halves(mids[i]), backward)
            for i in each:
                keep_wave(base + i).start()
            return carry

        lax.fori_loop(0, rounds, ready, 0)

        def kept(n, carry):
            keep_wave(n).wait()
            return carry

        lax.fori_loop(0, rounds * GROUP, kept, 0)
        for copy in posts:
            copy.wait()
        return
    stores = []

    def store(src, dst):
        copy = pltpu.make_async_copy(src, dst, load_sem.at[len(stores)])
        copy.start()
        stores.append(copy)

    for c in range(2):
        for j in range(strips):
            in_main = j < main_strips
            upper, lower = (out_main, out_bottom) if in_main else (out_right, out_corner)
            lanes = pl.ds((j if in_main else j - main_strips) * LANES, LANES)
            store(grad.at[c, j, pl.ds(0, tile)], upper.at[c, :, lanes])
            store(grad.at[c, j, pl.ds(tile, side)], lower.at[c, :, lanes])
    for t, (c, down, across) in enumerate(tiles_of(side)):
        probe_out[t] = probe[c, down, across]
    for copy in stores:
        copy.wait()


def add_chunk(meta, next_meta, pieces, illumination, tables, measured, so_far):
    main = pieces[0]
    tile, side = main.shape[1], illumination.shape[1]
    strips = (tile + side) // LANES
    grad_shape = (2, strips, tile + side, LANES)
    last_count = next_meta.shape[1]
    vmem = pl.BlockSpec(memory_space=pltpu.VMEM)
    smem = pl.BlockSpec(memory_space=pltpu.SMEM)
    hbm = pl.BlockSpec(memory_space=pltpu.HBM)
    both = (2, side, side)
    if so_far:
        sizes = [(2, tile, tile), (2, tile, side), (2, side, tile), both]
        sizes.append((2 * side * side // (8 * LANES), 8, LANES))
        out_specs = [hbm] * 4 + [vmem]
        held = 2 * GROUP
    else:
        sizes = [(2 * strips + 4, tile + side, LANES), (last_count, side, 2 * side)]
        out_specs = [hbm] * 2
        held = last_count
    count = meta.shape[1]
    return pl.pallas_call(
        functools.partial(grad_kernel, 1 if so_far else 0),
        out_shape=[jax.ShapeDtypeStruct(size, jnp.float32) for size in sizes],
        in_specs=[smem] * 2 + [hbm] * (9 if so_far else 8),
        out_specs=out_specs,
        scratch_shapes=[
            pltpu.VMEM(grad_shape, jnp.float32),
            pltpu.VMEM(grad_shape, jnp.float32),
            pltpu.VMEM(both, jnp.float32),
            pltpu.VMEM(both, jnp.float32),
            pltpu.VMEM(tables[0].shape, tables[0].dtype),
            pltpu.VMEM(tables[1].shape, tables[1].dtype),
            pltpu.VMEM((2 * GROUP, side, side), jnp.float32),
            pltpu.VMEM((held, side, 2 * side), jnp.float32),
            *[pltpu.VMEM(both, jnp.float32) for _ in range(GROUP)],
            pltpu.SMEM((max(count, last_count),), jnp.int32),
            pltpu.SemaphoreType.DMA((8 * strips,)),
            pltpu.SemaphoreType.DMA((2 * GROUP,)),
            pltpu.SemaphoreType.DMA((held,)),
        ],
        compiler_params=pltpu.CompilerParams(vmem_limit_bytes=48 * 2**20),
        cost_estimate=pl.CostEstimate(
            flops=count * 16 * 2 * side**3,
            bytes_accessed=count * 4 * side * side + 3 * 8 * (tile + side) ** 2,
            transcendentals=count * side * side,
        ),
    )(meta, next_meta, *pieces, *tables, measured, *(so_far or (illumination,)))


def tail_kernel(
    rows,
    cols,
    scale,
    right_ref,
    bottom_ref,
    corner_ref,
    probe_ref,
    got_right,
    got_bottom,
    probe_out,
    got_corner,
    right_top,
    part,
    row_sum,
    piece,
    total,
    gathered,
    whole_probe,
    top_sem,
    edge_send,
    edge_recv,
    row_send,
    row_recv,
    col_send,
    col_recv,
):
    r, c = lax.axis_index("row"), lax.axis_index("col")
    side = corner_ref.shape[1]
    below, right = lax.rem(r + 1, rows), lax.rem(c + 1, cols)
    top, rest = pl.ds(0, side), pl.ds(side, right_ref.shape[1] - side)
    top_copy = pltpu.make_async_copy(right_ref.at[:, top], right_top, top_sem)
    top_copy.start()
    barrier = pltpu.get_barrier_semaphore()
    for o in range(1, rows):
        pl.semaphore_signal(
            barrier, device_id=(lax.rem(r + o, rows), c), device_id_type=pl.DeviceIdType.MESH
        )
    for o in range(1, cols):
        pl.semaphore_signal(
            barrier, device_id=(r, lax.rem(c + o, cols)), device_id_type=pl.DeviceIdType.MESH
        )
    top_copy.wait()
    pl.semaphore_wait(barrier, rows + cols - 2)

    def send(src, dst, send_sem, recv_sem, device):
        copy = pltpu.make_async_remote_copy(
            src_ref=src,
            dst_ref=dst,
            send_sem=send_sem,
            recv_sem=recv_sem,
            device_id=device,
            device_id_type=pl.DeviceIdType.MESH,
        )
        copy.start()
        return copy

    first = []
    for o in range(1, rows):
        to = lax.rem(r + o, rows)
        first.append(
            send(probe_ref.at[to], part.at[o], row_send.at[0, o], row_recv.at[0, o], (to, c))
        )
    to_corner = send(corner_ref, got_corner, edge_send.at[0], edge_recv.at[0], (below, c))
    to_rest = send(
        right_ref.at[:, rest], got_right.at[:, rest], edge_send.at[1], edge_recv.at[1], (r, right)
    )
    summed = probe_ref[r]
    for o in range(1, rows):
        first[o - 1].wait_recv()
        summed = summed + part[o]
    row_sum[...] = summed
    second = []
    for o in range(1, cols):
        to = lax.rem(c + o, cols)
        second.append(
            send(row_sum.at[to], piece.at[o], col_send.at[0, o], col_recv.at[0, o], (r, to))
        )
    to_corner.wait()
    right_top[...] += got_corner[...]
    to_top = send(right_top, got_right.at[:, top], edge_send.at[3], edge_recv.at[3], (r, right))
    to_bottom = send(bottom_ref, got_bottom, edge_send.at[2], edge_recv.at[2], (below, c))
    whole = row_sum[c]
    for o in range(1, cols):
        second[o - 1].wait_recv()
        whole = whole + piece[o]
    total[...] = whole
    gathered[c] = whole
    third = []
    for o in range(1, cols):
        to = lax.rem(c + o, cols)
        third.append(
            send(total, gathered.at[c], col_send.at[1, o], col_recv.at[1, o], (r, to))
        )
    for copy in third:
        copy.wait_recv()
    whole_probe[r] = gathered[...]
    fourth = []
    for o in range(1, rows):
        to = lax.rem(r + o, rows)
        fourth.append(
            send(gathered, whole_probe.at[r], row_send.at[1, o], row_recv.at[1, o], (to, c))
        )
    for copy in fourth:
        copy.wait_recv()
    for t, (part_at, down, across) in enumerate(tiles_of(side)):
        probe_out[part_at, down, across] = whole_probe[t // cols, t % cols] * scale
    for copy in first + second + third + fourth:
        copy.wait_send()
    to_bottom.wait()
    to_rest.wait()
    to_top.wait()


def tail(right, bottom, corner, probe, rows, cols, scale):
    side = corner.shape[1]
    share = probe.shape[0] // (rows * cols) * 8
    vmem = pl.BlockSpec(memory_space=pltpu.VMEM)
    hbm = pl.BlockSpec(memory_space=pltpu.HBM)
    dma = pltpu.SemaphoreType.DMA
    split = (rows, cols, share, LANES)
    both = (2, side, side)
    return pl.pallas_call(
        functools.partial(tail_kernel, rows, cols, scale),
        out_shape=[
            jax.ShapeDtypeStruct(right.shape, jnp.float32),
            jax.ShapeDtypeStruct(bottom.shape, jnp.float32),
            jax.ShapeDtypeStruct(both, jnp.float32),
        ],
        in_specs=[hbm] * 3 + [vmem],
        out_specs=[vmem] * 3,
        scratch_shapes=[
            pltpu.VMEM(both, jnp.float32),
            pltpu.VMEM(both, jnp.float32),
            pltpu.VMEM(split, jnp.float32),
            pltpu.VMEM(split[1:], jnp.float32),
            pltpu.VMEM(split[1:], jnp.float32),
            pltpu.VMEM(split[2:], jnp.float32),
            pltpu.VMEM(split[1:], jnp.float32),
            pltpu.VMEM(split, jnp.float32),
            dma,
            dma((4,)),
            dma((4,)),
            dma((2, rows)),
            dma((2, rows)),
            dma((2, cols)),
            dma((2, cols)),
        ],
        compiler_params=pltpu.CompilerParams(
            collective_id=0, has_side_effects=True, vmem_limit_bytes=32 * 2**20
        ),
    )(right, bottom, corner, probe.reshape(split))


def on_device(object_field, illumination, positions, owners, intensities):
    tile = object_field.shape[1]
    side = illumination.shape[1]
    cols = lax.axis_size("col")
    row_count = lax.axis_size("row")
    pos_dev = positions.shape[0]
    band = lax.axis_index("row")
    column = lax.axis_index("col")
    limit_rows = row_count * tile - side
    limit_cols = cols * tile - side

    earlier = (jnp.arange(pos_dev)[:, None] < jnp.arange(pos_dev)[None, :]).astype(jnp.int32)

    def rank(same):
        return jnp.sum(same.astype(jnp.int32) * earlier, axis=-2)

    layer_of = rank(owners[:, None] == owners[None, :])
    columns = jnp.arange(cols, dtype=jnp.int32)
    layers = jnp.arange(CAP, dtype=jnp.int32)
    slot = (owners[:, None, None] == columns[:, None]) & (layer_of[:, None, None] == layers)
    slot = slot.astype(jnp.int32)
    request = [jnp.sum(slot * positions[:, i, None, None], axis=0) for i in range(2)]
    request = jnp.stack(request + [jnp.sum(slot, axis=0)])
    asks = jnp.moveaxis(request, 0, 1).reshape(cols, 1, 3 * CAP).astype(jnp.float32)
    asks = jnp.pad(asks, ((0, 0), (0, ASK_ROWS - 1), (0, side - 3 * CAP)))

    below = passed_along(object_field[:, :side, :], "row", -1)
    beside = passed_along(object_field[:, :, :side], "col", -1)
    pairs, lasts = pack(layer_of, owners, asks, intensities)
    pairs, lasts, beside, below = lax.optimization_barrier((pairs, lasts, beside, below))
    corner = passed_along(beside[:, :side, :], "row", -1)
    pieces = (object_field, below, beside, corner)

    t_re, t_im = dft_tables(side)
    tables = (
        jnp.block([[t_re, -t_im], [t_im, t_re]]),
        jnp.block([[t_re, t_im], [-t_im, t_re]]),
    )

    pairs = lax.all_to_all(pairs, "col", split_axis=0, concat_axis=0, tiled=True)
    lasts, pairs = lax.optimization_barrier((lasts, pairs))
    got = pairs[:, (CAP - 1) * side, : 3 * CAP].astype(jnp.int32).reshape(cols, 3, CAP)
    row_at = jnp.minimum(band * tile + got[:, 0], limit_rows) - band * tile
    col_at = jnp.minimum(column * tile + got[:, 1], limit_cols) - column * tile
    meta = jnp.stack([row_at, col_at, got[:, 2]])
    lasts = lax.all_to_all(lasts, "col", split_axis=0, concat_axis=0, tiled=True)
    last_meta = meta[:, :, CAP - 1]
    so_far = add_chunk(
        meta[:, :, : CAP - 1].reshape(3, -1), last_meta, pieces, illumination, tables, pairs, ()
    )
    main, right, bottom, corner, probe = add_chunk(
        last_meta, last_meta, pieces, illumination, tables, lasts, so_far
    )
    scale = 1.0 / math.sqrt(pos_dev * row_count * cols)
    from_left, from_above, probe_grad = tail(
        right, bottom, corner, probe, row_count, cols, scale
    )
    past = tile - side
    object_grad = (
        main
        + jnp.pad(from_left, ((0, 0), (0, 0), (0, past)))
        + jnp.pad(from_above, ((0, 0), (0, past), (0, 0)))
    )
    return (object_grad, probe_grad)


def solution(mesh):
    return jax.shard_map(
        on_device,
        mesh=mesh,
        in_specs=(
            P(None, "row", "col"),
            P(),
            P(("row", "col"), None),
            P(("row", "col")),
            P(("row", "col"), None, None),
        ),
        out_specs=(P(None, "row", "col"), P()),
        check_vma=False,
    )
```

```python
import functools
import math

import jax
import jax.numpy as jnp
from jax import lax
from jax.experimental import pallas as pl
from jax.experimental.pallas import tpu as pltpu
from jax.sharding import PartitionSpec as P

CAP = 3
LANES = 128
ASK_ROWS = 8
GROUP = 2


def passed_along(value, axis, steps):
    count = lax.axis_size(axis)
    leading, last = (max(0, -steps), min(count, count - steps))
    return lax.ppermute(value, axis, [(source, source + steps) for source in range(leading, last)])


def dft_tables(length):
    grid_ids = jnp.arange(length, dtype=jnp.int32)
    phase_ids = grid_ids[:, None] * grid_ids[None, :] % length
    angles = phase_ids.astype(jnp.float32) * (2.0 * math.pi / length)
    scale_factor = 1.0 / math.sqrt(length)
    return (
        (jnp.cos(angles) * scale_factor).astype(jnp.bfloat16),
        (-jnp.sin(angles) * scale_factor).astype(jnp.bfloat16),
    )


def pack_kernel(layer_ref, owner_ref, ask_ref, src_ref, pair_out, last_out, held, in_sem, out_sem):
    count, side = src_ref.shape[:2]
    asked = pltpu.make_async_copy(
        ask_ref, pair_out.at[:, pl.ds((CAP - 1) * side, ASK_ROWS)], out_sem.at[count]
    )
    asked.start()

    def copy_in(p):
        return pltpu.make_async_copy(src_ref.at[p], held.at[p], in_sem.at[p])

    def copy_pair(p):
        rows = pl.ds(pl.multiple_of(layer_ref[p] * side, side), side)
        return pltpu.make_async_copy(held.at[p], pair_out.at[owner_ref[p], rows], out_sem.at[p])

    def copy_last(p):
        return pltpu.make_async_copy(held.at[p], last_out.at[owner_ref[p]], out_sem.at[p])

    for p in range(count):
        copy_in(p).start()
    for p in range(count):
        copy_in(p).wait()
        last = layer_ref[p] == CAP - 1

        @pl.when(last)
        def _():
            copy_last(p).start()

        @pl.when(jnp.logical_not(last))
        def _():
            copy_pair(p).start()

    for p in range(count):
        copy_last(p).wait()
    asked.wait()


def pack(layer_of, owners, asks, intensities):
    count, side = intensities.shape[:2]
    cols = asks.shape[0]
    smem = pl.BlockSpec(memory_space=pltpu.SMEM)
    hbm = pl.BlockSpec(memory_space=pltpu.HBM)
    return pl.pallas_call(
        pack_kernel,
        out_shape=[
            jax.ShapeDtypeStruct((cols, (CAP - 1) * side + ASK_ROWS, side), jnp.float32),
            jax.ShapeDtypeStruct((cols, side, side), jnp.float32),
        ],
        in_specs=[smem, smem, hbm, hbm],
        out_specs=[hbm, hbm],
        scratch_shapes=[
            pltpu.VMEM(intensities.shape, jnp.float32),
            pltpu.SemaphoreType.DMA((count,)),
            pltpu.SemaphoreType.DMA((count + 1,)),
        ],
        compiler_params=pltpu.CompilerParams(vmem_limit_bytes=24 * 2**20),
        cost_estimate=pl.CostEstimate(
            flops=0, bytes_accessed=2 * intensities.size * 4, transcendentals=0
        ),
    )(layer_of, owners, asks, intensities)


def dot(first, second):
    return jnp.dot(first, second, preferred_element_type=jnp.float32)


def mm(first, second):
    if first.shape[0] == first.shape[1]:
        half = first.shape[0] // 2
        return jnp.concatenate([dot(first[:half], second), dot(first[half:], second)], axis=0)
    half = second.shape[1] // 2
    return jnp.concatenate([dot(first, second[:, :half]), dot(first, second[:, half:])], axis=1)


def tiles_of(side):
    return [
        (c, pl.ds(i, 8), pl.ds(j, LANES))
        for c in range(2)
        for i in range(0, side, 8)
        for j in range(0, side, LANES)
    ]


def grad_kernel(
    phase,
    meta_ref,
    next_ref,
    main_ref,
    below_ref,
    beside_ref,
    corner_ref,
    left_in,
    right_in,
    meas_ref,
    *refs,
):
    if phase == 0:
        illum_in, grad_out, waves_out, *refs = refs
    else:
        (
            grad_in,
            waves_in,
            out_main,
            out_right,
            out_bottom,
            out_corner,
            probe_out,
            *refs,
        ) = refs
    ext, grad, probe, illum_ref, left_ref, right_ref, meas, waves, *refs = refs
    patches, (live_list, load_sem, meas_sem, wave_sem) = refs[:GROUP], refs[GROUP:]
    tile = main_ref.shape[1]
    side = illum_ref.shape[1]
    strips = ext.shape[1]
    main_strips = tile // LANES
    slots = meta_ref.shape[1]
    loads = []

    def load(src, dst):
        copy = pltpu.make_async_copy(src, dst, load_sem.at[len(loads)])
        copy.start()
        loads.append(copy)

    both_strips = [(c, j) for c in range(2) for j in range(side // LANES)]
    held_at = [(c, pl.ds(j * side, side)) for c, j in both_strips]
    if phase == 0:
        load(illum_in, illum_ref)
    load(left_in, left_ref)
    load(right_in, right_ref)
    for c in range(2):
        for j in range(main_strips):
            lanes = pl.ds(j * LANES, LANES)
            load(main_ref.at[c, :, lanes], ext.at[c, j, pl.ds(0, tile)])
            load(below_ref.at[c, :, lanes], ext.at[c, j, pl.ds(tile, side)])
        for j in range(strips - main_strips):
            lanes = pl.ds(j * LANES, LANES)
            load(beside_ref.at[c, :, lanes], ext.at[c, main_strips + j, pl.ds(0, tile)])
            load(corner_ref.at[c, :, lanes], ext.at[c, main_strips + j, pl.ds(tile, side)])
    if phase == 0:
        grad[...] = jnp.zeros(grad.shape, grad.dtype)
        probe[...] = jnp.zeros(probe.shape, probe.dtype)
    else:
        for (c, j), (at, rows) in zip(both_strips, held_at):
            lanes = pl.ds(j * LANES, LANES)
            load(grad_in.at[2 * strips + at, rows], probe.at[c, :, lanes])
            load(grad_in.at[2 * strips + 2 + at, rows], illum_ref.at[c, :, lanes])
        for c in range(2):
            load(grad_in.at[pl.ds(c * strips, strips)], grad.at[c])

    def list_live(layer_ref):
        def gather_live(s, n):
            alive = layer_ref[2, s] > 0

            @pl.when(alive)
            def _():
                live_list[n] = s

            return n + alive.astype(jnp.int32)

        return lax.fori_loop(0, layer_ref.shape[1], gather_live, jnp.int32(0))

    total = list_live(meta_ref)

    def fetch(n):
        slot = n % (2 * GROUP)
        at = jnp.minimum(n, total - 1)
        place = live_list[at]
        if phase == 0:
            source = place // (CAP - 1)
            layer = place - source * (CAP - 1)
            found = meas_ref.at[source, pl.ds(pl.multiple_of(layer * side, side), side)]
        else:
            found = meas_ref.at[place]
        copies = [pltpu.make_async_copy(found, meas.at[slot], meas_sem.at[slot])]
        if phase > 0:
            copies.append(
                pltpu.make_async_copy(waves_in.at[at], waves.at[slot], wave_sem.at[slot])
            )
        return copies

    @pl.when(total > 0)
    def _():
        for i in range(GROUP):
            for copy in fetch(i):
                copy.start()

    for copy in loads:
        copy.wait()

    lane = lax.broadcasted_iota(jnp.int32, (side, LANES), 1)
    each = range(GROUP)
    il_re, il_im = illum_ref[0], illum_ref[1]

    def places_of(layer_ref, base, count):
        places = []
        for i in each:
            s = live_list[jnp.minimum(base + i, count - 1)]
            col = layer_ref[1, s]
            strip = col // LANES
            places.append((pl.ds(layer_ref[0, s], side), strip, col - strip * LANES))
        return places

    def patch_of(place):
        rows, strip, shift = place
        back_shift = (LANES - shift) % LANES
        keep = lane < LANES - shift
        patch = []
        for c in range(2):
            rolled = [pltpu.roll(ext[c, strip + t, rows, :], back_shift, 1) for t in range(3)]
            whole = [jnp.where(keep, rolled[t], rolled[t + 1]) for t in range(2)]
            patch.append(jnp.concatenate(whole, axis=1))
        return patch

    def exit_of(patch):
        pa_re, pa_im = patch
        parts = [il_re * pa_re - il_im * pa_im, il_re * pa_im + il_im * pa_re]
        return jnp.concatenate([part.astype(jnp.bfloat16) for part in parts], axis=0)

    def halves(stage):
        return jnp.concatenate([stage[:side], stage[side:]], axis=1)

    def step(g, carry):
        base = g * GROUP

        @pl.when((g + 1) * GROUP < total)
        def _():
            for i in each:
                for copy in fetch(base + GROUP + i):
                    copy.start()

        for i in each:
            for copy in fetch(base + i):
                copy.wait()
        places = places_of(meta_ref, base, total)
        weights = [jnp.where(base + i < total, 1.0, 0.0) for i in each]
        forward, backward = left_ref[...], right_ref[...]

        def residual(i, wave):
            w_re, w_im = wave[:, :side], wave[:, side:]
            measured = meas[(base + i) % (2 * GROUP)]
            power = jnp.maximum(w_re * w_re + w_im * w_im, 0.25)
            factor = 1.0 - measured * lax.rsqrt(measured * power)
            if i > 0:
                factor = factor * weights[i]
            parts = [(w_re * factor).astype(jnp.bfloat16), (w_im * factor).astype(jnp.bfloat16)]
            return jnp.concatenate(parts, axis=0)

        def leave(i, back):
            rows, strip, shift = places[i]
            b_re, b_im = back[:, :side], back[:, side:]
            if phase == 0:
                pa_re, pa_im = patches[i][0], patches[i][1]
            else:
                pa_re, pa_im = patch_of(places[i])
            terms = (il_re * b_re + il_im * b_im, il_re * b_im - il_im * b_re)
            early = lane < shift
            for c in range(2):
                one = pltpu.roll(terms[c][:, :LANES], shift, 1)
                two = pltpu.roll(terms[c][:, LANES:], shift, 1)
                grad[c, strip, rows, :] += jnp.where(early, 0.0, one)
                grad[c, strip + 1, rows, :] += jnp.where(early, one, two)
                grad[c, strip + 2, rows, :] += jnp.where(early, two, 0.0)
            return pa_re * b_re + pa_im * b_im, pa_re * b_im - pa_im * b_re

        if phase == 0:
            exits = []
            for i in each:
                patch = patch_of(places[i])
                patches[i][0], patches[i][1] = patch
                exits.append(exit_of(patch))
            mids = [mm(forward, exits[i]).astype(jnp.bfloat16) for i in each]
            diffs = [residual(i, mm(halves(mids[i]), backward)) for i in each]
        else:
            diffs = [residual(i, waves[(base + i) % (2 * GROUP)]) for i in each]
        mids = [mm(backward, diffs[i]).astype(jnp.bfloat16) for i in each]
        terms = [leave(i, mm(halves(mids[i]), forward)) for i in each]
        probe[0] += sum(term[0] for term in terms)
        probe[1] += sum(term[1] for term in terms)
        return carry

    lax.fori_loop(0, (total + GROUP - 1) // GROUP, step, 0)
    if phase == 0:
        posts = []

        def post(src, dst):
            copy = pltpu.make_async_copy(src, dst, load_sem.at[len(posts)])
            copy.start()
            posts.append(copy)

        for c in range(2):
            post(grad.at[c], grad_out.at[pl.ds(c * strips, strips)])
        for (c, j), (at, rows) in zip(both_strips, held_at):
            lanes = pl.ds(j * LANES, LANES)
            post(probe.at[c, :, lanes], grad_out.at[2 * strips + at, rows])
            post(illum_ref.at[c, :, lanes], grad_out.at[2 * strips + 2 + at, rows])
        after = list_live(next_ref)
        rounds = (after + GROUP - 1) // GROUP

        def keep_wave(n):
            return pltpu.make_async_copy(waves.at[n], waves_out.at[n], wave_sem.at[n])

        def ready(g, carry):
            base = g * GROUP
            places = places_of(next_ref, base, after)
            forward, backward = left_ref[...], right_ref[...]
            exits = [exit_of(patch_of(places[i])) for i in each]
            mids = [mm(forward, exits[i]).astype(jnp.bfloat16) for i in each]
            for i in each:
                waves[base + i] = mm(halves(mids[i]), backward)
            for i in each:
                keep_wave(base + i).start()
            return carry

        lax.fori_loop(0, rounds, ready, 0)

        def kept(n, carry):
            keep_wave(n).wait()
            return carry

        lax.fori_loop(0, rounds * GROUP, kept, 0)
        for copy in posts:
            copy.wait()
        return
    stores = []

    def store(src, dst):
        copy = pltpu.make_async_copy(src, dst, load_sem.at[len(stores)])
        copy.start()
        stores.append(copy)

    for c in range(2):
        for j in range(strips):
            in_main = j < main_strips
            upper, lower = (out_main, out_bottom) if in_main else (out_right, out_corner)
            lanes = pl.ds((j if in_main else j - main_strips) * LANES, LANES)
            store(grad.at[c, j, pl.ds(0, tile)], upper.at[c, :, lanes])
            store(grad.at[c, j, pl.ds(tile, side)], lower.at[c, :, lanes])
    for t, (c, down, across) in enumerate(tiles_of(side)):
        probe_out[t] = probe[c, down, across]
    for copy in stores:
        copy.wait()


def add_chunk(meta, next_meta, pieces, illumination, tables, measured, so_far):
    main = pieces[0]
    tile, side = main.shape[1], illumination.shape[1]
    strips = (tile + side) // LANES
    grad_shape = (2, strips, tile + side, LANES)
    last_count = next_meta.shape[1]
    vmem = pl.BlockSpec(memory_space=pltpu.VMEM)
    smem = pl.BlockSpec(memory_space=pltpu.SMEM)
    hbm = pl.BlockSpec(memory_space=pltpu.HBM)
    both = (2, side, side)
    if so_far:
        sizes = [(2, tile, tile), (2, tile, side), (2, side, tile), both]
        sizes.append((2 * side * side // (8 * LANES), 8, LANES))
        out_specs = [hbm] * 4 + [vmem]
        held = 2 * GROUP
    else:
        sizes = [(2 * strips + 4, tile + side, LANES), (last_count, side, 2 * side)]
        out_specs = [hbm] * 2
        held = last_count
    count = meta.shape[1]
    return pl.pallas_call(
        functools.partial(grad_kernel, 1 if so_far else 0),
        out_shape=[jax.ShapeDtypeStruct(size, jnp.float32) for size in sizes],
        in_specs=[smem] * 2 + [hbm] * (9 if so_far else 8),
        out_specs=out_specs,
        scratch_shapes=[
            pltpu.VMEM(grad_shape, jnp.float32),
            pltpu.VMEM(grad_shape, jnp.float32),
            pltpu.VMEM(both, jnp.float32),
            pltpu.VMEM(both, jnp.float32),
            pltpu.VMEM(tables[0].shape, tables[0].dtype),
            pltpu.VMEM(tables[1].shape, tables[1].dtype),
            pltpu.VMEM((2 * GROUP, side, side), jnp.float32),
            pltpu.VMEM((held, side, 2 * side), jnp.float32),
            *[pltpu.VMEM(both, jnp.float32) for _ in range(GROUP)],
            pltpu.SMEM((max(count, last_count),), jnp.int32),
            pltpu.SemaphoreType.DMA((8 * strips,)),
            pltpu.SemaphoreType.DMA((2 * GROUP,)),
            pltpu.SemaphoreType.DMA((held,)),
        ],
        compiler_params=pltpu.CompilerParams(vmem_limit_bytes=48 * 2**20),
        cost_estimate=pl.CostEstimate(
            flops=count * 16 * 2 * side**3,
            bytes_accessed=count * 4 * side * side + 3 * 8 * (tile + side) ** 2,
            transcendentals=count * side * side,
        ),
    )(meta, next_meta, *pieces, *tables, measured, *(so_far or (illumination,)))


def tail_kernel(
    rows,
    cols,
    scale,
    right_ref,
    bottom_ref,
    corner_ref,
    probe_ref,
    got_right,
    got_bottom,
    probe_out,
    got_corner,
    right_top,
    part,
    row_sum,
    piece,
    total,
    gathered,
    whole_probe,
    top_sem,
    edge_send,
    edge_recv,
    row_send,
    row_recv,
    col_send,
    col_recv,
):
    r, c = lax.axis_index("row"), lax.axis_index("col")
    side = corner_ref.shape[1]
    below, right = lax.rem(r + 1, rows), lax.rem(c + 1, cols)
    top, rest = pl.ds(0, side), pl.ds(side, right_ref.shape[1] - side)
    top_copy = pltpu.make_async_copy(right_ref.at[:, top], right_top, top_sem)
    top_copy.start()
    barrier = pltpu.get_barrier_semaphore()
    for o in range(1, rows):
        pl.semaphore_signal(
            barrier, device_id=(lax.rem(r + o, rows), c), device_id_type=pl.DeviceIdType.MESH
        )
    for o in range(1, cols):
        pl.semaphore_signal(
            barrier, device_id=(r, lax.rem(c + o, cols)), device_id_type=pl.DeviceIdType.MESH
        )
    top_copy.wait()
    pl.semaphore_wait(barrier, rows + cols - 2)

    def send(src, dst, send_sem, recv_sem, device):
        copy = pltpu.make_async_remote_copy(
            src_ref=src,
            dst_ref=dst,
            send_sem=send_sem,
            recv_sem=recv_sem,
            device_id=device,
            device_id_type=pl.DeviceIdType.MESH,
        )
        copy.start()
        return copy

    first = []
    for o in range(1, rows):
        to = lax.rem(r + o, rows)
        first.append(
            send(probe_ref.at[to], part.at[o], row_send.at[0, o], row_recv.at[0, o], (to, c))
        )
    to_corner = send(corner_ref, got_corner, edge_send.at[0], edge_recv.at[0], (below, c))
    to_rest = send(
        right_ref.at[:, rest], got_right.at[:, rest], edge_send.at[1], edge_recv.at[1], (r, right)
    )
    summed = probe_ref[r]
    for o in range(1, rows):
        first[o - 1].wait_recv()
        summed = summed + part[o]
    row_sum[...] = summed
    second = []
    for o in range(1, cols):
        to = lax.rem(c + o, cols)
        second.append(
            send(row_sum.at[to], piece.at[o], col_send.at[0, o], col_recv.at[0, o], (r, to))
        )
    to_corner.wait()
    right_top[...] += got_corner[...]
    to_top = send(right_top, got_right.at[:, top], edge_send.at[3], edge_recv.at[3], (r, right))
    to_bottom = send(bottom_ref, got_bottom, edge_send.at[2], edge_recv.at[2], (below, c))
    whole = row_sum[c]
    for o in range(1, cols):
        second[o - 1].wait_recv()
        whole = whole + piece[o]
    total[...] = whole
    gathered[c] = whole
    third = []
    for o in range(1, cols):
        to = lax.rem(c + o, cols)
        third.append(
            send(total, gathered.at[c], col_send.at[1, o], col_recv.at[1, o], (r, to))
        )
    for copy in third:
        copy.wait_recv()
    whole_probe[r] = gathered[...]
    fourth = []
    for o in range(1, rows):
        to = lax.rem(r + o, rows)
        fourth.append(
            send(gathered, whole_probe.at[r], row_send.at[1, o], row_recv.at[1, o], (to, c))
        )
    for copy in fourth:
        copy.wait_recv()
    for t, (part_at, down, across) in enumerate(tiles_of(side)):
        probe_out[part_at, down, across] = whole_probe[t // cols, t % cols] * scale
    for copy in first + second + third + fourth:
        copy.wait_send()
    to_bottom.wait()
    to_rest.wait()
    to_top.wait()


def tail(right, bottom, corner, probe, rows, cols, scale):
    side = corner.shape[1]
    share = probe.shape[0] // (rows * cols) * 8
    vmem = pl.BlockSpec(memory_space=pltpu.VMEM)
    hbm = pl.BlockSpec(memory_space=pltpu.HBM)
    dma = pltpu.SemaphoreType.DMA
    split = (rows, cols, share, LANES)
    both = (2, side, side)
    return pl.pallas_call(
        functools.partial(tail_kernel, rows, cols, scale),
        out_shape=[
            jax.ShapeDtypeStruct(right.shape, jnp.float32),
            jax.ShapeDtypeStruct(bottom.shape, jnp.float32),
            jax.ShapeDtypeStruct(both, jnp.float32),
        ],
        in_specs=[hbm] * 3 + [vmem],
        out_specs=[vmem] * 3,
        scratch_shapes=[
            pltpu.VMEM(both, jnp.float32),
            pltpu.VMEM(both, jnp.float32),
            pltpu.VMEM(split, jnp.float32),
            pltpu.VMEM(split[1:], jnp.float32),
            pltpu.VMEM(split[1:], jnp.float32),
            pltpu.VMEM(split[2:], jnp.float32),
            pltpu.VMEM(split[1:], jnp.float32),
            pltpu.VMEM(split, jnp.float32),
            dma,
            dma((4,)),
            dma((4,)),
            dma((2, rows)),
            dma((2, rows)),
            dma((2, cols)),
            dma((2, cols)),
        ],
        compiler_params=pltpu.CompilerParams(
            collective_id=0, has_side_effects=True, vmem_limit_bytes=32 * 2**20
        ),
    )(right, bottom, corner, probe.reshape(split))


def on_device(object_field, illumination, positions, owners, intensities):
    tile = object_field.shape[1]
    side = illumination.shape[1]
    cols = lax.axis_size("col")
    row_count = lax.axis_size("row")
    pos_dev = positions.shape[0]
    band = lax.axis_index("row")
    column = lax.axis_index("col")
    limit_rows = row_count * tile - side
    limit_cols = cols * tile - side

    earlier = (jnp.arange(pos_dev)[:, None] < jnp.arange(pos_dev)[None, :]).astype(jnp.int32)

    def rank(same):
        return jnp.sum(same.astype(jnp.int32) * earlier, axis=-2)

    layer_of = rank(owners[:, None] == owners[None, :])
    columns = jnp.arange(cols, dtype=jnp.int32)
    layers = jnp.arange(CAP, dtype=jnp.int32)
    slot = (owners[:, None, None] == columns[:, None]) & (layer_of[:, None, None] == layers)
    slot = slot.astype(jnp.int32)
    request = [jnp.sum(slot * positions[:, i, None, None], axis=0) for i in range(2)]
    request = jnp.stack(request + [jnp.sum(slot, axis=0)])
    asks = jnp.moveaxis(request, 0, 1).reshape(cols, 1, 3 * CAP).astype(jnp.float32)
    asks = jnp.pad(asks, ((0, 0), (0, ASK_ROWS - 1), (0, side - 3 * CAP)))

    below = passed_along(object_field[:, :side, :], "row", -1)
    beside = passed_along(object_field[:, :, :side], "col", -1)
    pairs, lasts = pack(layer_of, owners, asks, intensities)
    t_re, t_im = dft_tables(side)
    tables = (
        jnp.block([[t_re, -t_im], [t_im, t_re]]),
        jnp.block([[t_re, t_im], [-t_im, t_re]]),
    )
    pairs, lasts, beside, below, tables = lax.optimization_barrier(
        (pairs, lasts, beside, below, tables)
    )
    corner = passed_along(beside[:, :side, :], "row", -1)
    pieces = (object_field, below, beside, corner)

    pairs = lax.all_to_all(pairs, "col", split_axis=0, concat_axis=0, tiled=True)
    lasts, pairs = lax.optimization_barrier((lasts, pairs))
    got = pairs[:, (CAP - 1) * side, : 3 * CAP].astype(jnp.int32).reshape(cols, 3, CAP)
    row_at = jnp.minimum(band * tile + got[:, 0], limit_rows) - band * tile
    col_at = jnp.minimum(column * tile + got[:, 1], limit_cols) - column * tile
    meta = jnp.stack([row_at, col_at, got[:, 2]])
    lasts = lax.all_to_all(lasts, "col", split_axis=0, concat_axis=0, tiled=True)
    last_meta = meta[:, :, CAP - 1]
    so_far = add_chunk(
        meta[:, :, : CAP - 1].reshape(3, -1), last_meta, pieces, illumination, tables, pairs, ()
    )
    main, right, bottom, corner, probe = add_chunk(
        last_meta, last_meta, pieces, illumination, tables, lasts, so_far
    )
    scale = 1.0 / math.sqrt(pos_dev * row_count * cols)
    from_left, from_above, probe_grad = tail(
        right, bottom, corner, probe, row_count, cols, scale
    )
    past = tile - side
    object_grad = (
        main
        + jnp.pad(from_left, ((0, 0), (0, 0), (0, past)))
        + jnp.pad(from_above, ((0, 0), (0, past), (0, 0)))
    )
    return (object_grad, probe_grad)


def solution(mesh):
    return jax.shard_map(
        on_device,
        mesh=mesh,
        in_specs=(
            P(None, "row", "col"),
            P(),
            P(("row", "col"), None),
            P(("row", "col")),
            P(("row", "col"), None, None),
        ),
        out_specs=(P(None, "row", "col"), P()),
        check_vma=False,
    )
```
